256 devices in a mesh: dp: 4 (over z_lo), din: 8 (over y, core), dout: 8 (over z_hi, x).
Axes of the slice: x: 4, y: 4, z: 8 (z_hi: 2, z_lo: 4; z = z_hi * 4 + z_lo), core: 2. Of those that a mesh axis runs over, the one named last changes fastest.
Arguments:
- tokens: bfloat16 [1024, 8192], P(('dp', 'dout'), 'din'), may hold values from -6 to 6
- out_grad: bfloat16 [1024, 8192], P(('dp', 'dout'), 'din'), may hold values from -6 to 6
- gate_weight: bfloat16 [8192, 15360], P('din', 'dout'), may hold values from -0.0625 to 0.0625
- up_weight: bfloat16 [8192, 15360], P('din', 'dout'), may hold values from -0.0625 to 0.0625
- down_weight: bfloat16 [15360, 8192], P('dout', 'din'), may hold values from -0.046875 to 0.046875
- gate_step: float32 [15360], P('dout'), may hold values from 0.0027621358 to 0.011048543
- up_step: float32 [15360], P('dout'), may hold values from 0.0027621358 to 0.011048543
- down_step: float32 [8192], P('din'), may hold values from 0.0020171788 to 0.008068715
- outlier_in: int32 [128], P('din'), may hold values from 0 to 8191, as said below
- outlier_hidden: int32 [128], P('dout'), may hold values from 0 to 15359, as said below
Outputs:
- d_tokens: bfloat16 [1024, 8192], P(('dp', 'dout'), 'din')
- gate_step_grad: float32 [15360], P('dout')
- up_step_grad: float32 [15360], P('dout')
- down_step_grad: float32 [8192], P('din')
The draws below stay inside these ranges and needn't reach their ends.
Inputs may be any that keep to these rules, and one draw needn't show every extreme that they name: `outlier_in`: sorted ascending and distinct; exactly 16 of them in each aligned block of 1024 channels. `outlier_hidden`: sorted ascending and distinct; exactly 16 of them in each aligned block of 1920 hidden units.
All inputs are finite; a program needn't handle non-finite values.
Results may differ from the reference program's by a relative error of at most 0.0072.
Values may be sent and summed in bfloat16 or wider, within the bound.
A program may use at most 128 MiB of HBM per device.

```python
import math
import jax
import jax.numpy as jnp
from jax import lax

D = 8192
FF = 15360
TOK_DEV = 256
K_IN = 16
K_HID = 16
TOKENS = 1024
BLK_IN = 1024
BLK_HID = 1920
OUT_IN = 128
OUT_HID = 128


def pick_outliers(seed_key, per_block, block_size, block_total):
    ranking = jax.random.randint(seed_key, (block_total, block_size), 0, 1 << 16) * block_size + jnp.arange(block_size, dtype=jnp.int32)[None, :]
    top_rows = lax.top_k(ranking, per_block)[1].astype(jnp.int32)
    ordered = jnp.sort(top_rows, axis=1) + (jnp.arange(block_total, dtype=jnp.int32) * block_size)[:, None]
    return ordered.reshape(-1).astype(jnp.int32)


def draw_outlier_in(key, part):
    key = jax.random.fold_in(key, 1)
    return pick_outliers(key, K_IN, BLK_IN, OUT_IN // K_IN)


def draw_outlier_hidden(key, part):
    key = jax.random.fold_in(key, 2)
    return pick_outliers(key, K_HID, BLK_HID, OUT_HID // K_HID)


def block_levels(own_key, extent, pieces, low, high):
    loudness, own = 1.0, jax.random.fold_in(own_key, 6)
    for axis_at, parts in pieces:
        heights = jnp.exp(jax.random.uniform(jax.random.fold_in(own, axis_at), (parts,), jnp.float32, low / len(pieces), high / len(pieces)))
        loudness = loudness * jnp.repeat(heights, extent[axis_at] // parts).reshape([-1 if axis == axis_at else 1 for axis in range(len(extent))])
    return loudness


def centred(key, extent, width, most, shards=(), kind=jnp.bfloat16):
    drawn = jax.random.normal(key, extent, jnp.float32) * width
    if len(shards) > 0:
        drawn = block_levels(key, extent, shards, -0.22, 0.18) * drawn
    return jnp.clip(drawn, min=-most, max=most).astype(kind)


def setup_inputs(seed: int = 0) -> dict:
    key_of = jax.random.split(jax.random.key(seed), 11)
    return {
        "tokens": centred(key_of[0], (TOKENS, D), 1.0, 6.0, ((0, 32), (1, 8))),
        "out_grad": centred(key_of[1], (TOKENS, D), 1.0, 6.0, ((0, 32), (1, 8))),
        "gate_weight": centred(key_of[2], (D, FF), D ** -0.5, 0.0625, ((0, 8), (1, 8))),
        "up_weight": centred(key_of[3], (D, FF), D ** -0.5, 0.0625, ((0, 8), (1, 8))),
        "down_weight": centred(key_of[4], (FF, D), FF ** -0.5, 0.046875, ((0, 8), (1, 8))),
        "gate_step": jnp.clip(jnp.exp(math.log(0.011048543) - 1.3862944 * jax.random.uniform(key_of[5], (FF,), jnp.float32) ** block_levels(key_of[5], (FF,), ((0, 8),), -0.2, 0.2)), 0.0027621358, 0.011048543),
        "up_step": jnp.clip(jnp.exp(math.log(0.011048543) - 1.3862944 * jax.random.uniform(key_of[6], (FF,), jnp.float32) ** block_levels(key_of[6], (FF,), ((0, 8),), -0.2, 0.2)), 0.0027621358, 0.011048543),
        "down_step": jnp.clip(jnp.exp(math.log(0.008068715) - 1.3862944 * jax.random.uniform(key_of[7], (D,), jnp.float32) ** block_levels(key_of[7], (D,), ((0, 8),), -0.2, 0.2)), 0.0020171788, 0.008068715),
        "outlier_in": draw_outlier_in(jax.random.fold_in(key_of[10], 71), 0),
        "outlier_hidden": draw_outlier_hidden(jax.random.fold_in(key_of[10], 71), 0),
    }


QUANT_TOP = 7.0
SOFT_ROUND = 0.9
FULL_TURN = 2.0 * math.pi

def soft_quant(weight, step_size, keep_rows):
    ratio = weight.astype(jnp.float32) / step_size[None, :]
    squash = jnp.tanh(ratio / QUANT_TOP)
    level_value = QUANT_TOP * squash
    phase_angle = FULL_TURN * level_value
    shaped = level_value - SOFT_ROUND * jnp.sin(phase_angle) / FULL_TURN
    slope_value = (1.0 - SOFT_ROUND * jnp.cos(phase_angle)) * (1.0 - squash * squash)
    quantized = jnp.where(keep_rows[:, None], weight.astype(jnp.float32), step_size[None, :] * shaped).astype(jnp.bfloat16)
    factor = jnp.where(keep_rows[:, None], jnp.float32(0.0), shaped - ratio * slope_value).astype(jnp.bfloat16)
    return (quantized, factor)

def reference(tokens, out_grad, gate_weight, up_weight, down_weight, gate_step, up_step, down_step, outlier_in, outlier_hidden):
    keep_in = jnp.any(jnp.arange(D, dtype=jnp.int32)[:, None] == outlier_in[None, :], axis=1)
    keep_hidden = jnp.any(jnp.arange(FF, dtype=jnp.int32)[:, None] == outlier_hidden[None, :], axis=1)
    q_gate, f_gate = soft_quant(gate_weight, gate_step, keep_in)
    q_up, f_up = soft_quant(up_weight, up_step, keep_in)
    q_down, f_down = soft_quant(down_weight, down_step, keep_hidden)
    gate_pre = jnp.dot(tokens, q_gate, preferred_element_type=jnp.float32)
    up_pre = jnp.dot(tokens, q_up, preferred_element_type=jnp.float32)
    back_grad = jnp.dot(out_grad, q_down.T, preferred_element_type=jnp.float32)
    logistic = jax.nn.sigmoid(gate_pre)
    d_gate = (back_grad * up_pre * logistic * (1.0 + gate_pre * (1.0 - logistic))).astype(jnp.bfloat16)
    d_up = (back_grad * gate_pre * logistic).astype(jnp.bfloat16)
    hidden = (gate_pre * logistic * up_pre).astype(jnp.bfloat16)
    d_tokens = (jnp.dot(d_gate, q_gate.T, preferred_element_type=jnp.float32) + jnp.dot(d_up, q_up.T, preferred_element_type=jnp.float32)).astype(jnp.bfloat16)
    scale_in = 1.0 / math.sqrt(D * TOK_DEV)
    scale_hidden = 1.0 / math.sqrt(FF * TOK_DEV)
    gate_step_grad = lax.optimization_barrier(jnp.sum(d_gate.astype(jnp.float32) * jnp.dot(tokens, f_gate, preferred_element_type=jnp.float32), axis=0)) * scale_in
    up_step_grad = lax.optimization_barrier(jnp.sum(d_up.astype(jnp.float32) * jnp.dot(tokens, f_up, preferred_element_type=jnp.float32), axis=0)) * scale_in
    down_step_grad = lax.optimization_barrier(jnp.sum(out_grad.astype(jnp.float32) * jnp.dot(hidden, f_down, preferred_element_type=jnp.float32), axis=0)) * scale_hidden
    return (d_tokens, gate_step_grad, up_step_grad, down_step_grad)
```

```python
import math

import jax
import jax.numpy as jnp
from jax import lax
from jax.experimental import pallas as pl
from jax.experimental.pallas import tpu as pltpu
from jax.sharding import PartitionSpec as P

D = 8192
FF = 15360
TOK_DEV = 256
SCALE_IN = 1.0 / math.sqrt(D * TOK_DEV)
SCALE_HID = 1.0 / math.sqrt(FF * TOK_DEV)

KB = 1024
HB = 1920
N = 5
C = HB // N
C2, C3 = 2 * C, 3 * C
T = 256
HALF = T // 2
BLK = 32

MESH = pl.DeviceIdType.MESH
BF, F32 = jnp.bfloat16, jnp.float32

SIN = (3.14158202, -5.16714276, 2.5418987, -0.55463534)


def quant(w, step, inv7, keep):
    w = w.astype(F32)
    x = w * inv7
    t = jnp.tanh(x)
    c = 7.0 * t
    r = c - jnp.round(c)
    u = r * r
    p = jnp.float32(SIN[3])
    for k in (2, 1, 0):
        p = p * u + jnp.float32(SIN[k])
    sn = p * r
    s2 = sn * sn
    d = jnp.maximum(1.0 - s2, 1e-12)
    cs = d * lax.rsqrt(d)
    shaped = c - sn * cs * jnp.float32(0.9 / math.pi)
    slope7 = (0.7 + 12.6 * s2) * (1.0 - t * t)
    q = jnp.where(keep, w, step * shaped)
    f = jnp.where(keep, 0.0, shaped - x * slope7)
    return q.astype(BF), f.astype(BF)


def remote(src, dst, ssem, rsem, dev):
    return pltpu.make_async_remote_copy(
        src_ref=src, dst_ref=dst, send_sem=ssem, recv_sem=rsem, device_id=dev, device_id_type=MESH
    )


def dot(a, b):
    return jnp.dot(a, b, preferred_element_type=F32)


def dot_t(a, b):
    return lax.dot_general(a, b, (((1,), (1,)), ((), ())), preferred_element_type=F32)


def kernel(
    tok_hbm, og_hbm, gw, uw, dw, gs, us, ds, oi, oh,
    dt_out, gg_out, ug_out, dg_out,
    tg, wgu, fgu, wd, fd, kin, khid, sgu, igu, idn,
    pre, send1, recv1, send2, recv2, act,
    acc, esend, erecv, gt, gslot, gdp, dterm, dslot, dz,
    lsem, gusem, dsem, zs, zr, xs, xr, s1s, s1r, y2s, y2r, ags, agr, s2s, s2r,
    es, er, gs_s, gs_r, gp_s, gp_r, ds_s, ds_r, dz_s, dz_r,
):
    dp = lax.axis_index("dp")
    din = lax.axis_index("din")
    dout = lax.axis_index("dout")
    y, c = din // 2, din % 2
    zh, x = dout // 4, dout % 4

    def at_y(k, core):
        return (dp, (k % 4) * 2 + core, dout)

    def at_x(k, hi):
        return (dp, din, hi * 4 + k % 4)

    sibling = (dp, y * 2 + (1 - c), dout)

    def rows_of(block):
        return pl.ds(pl.multiple_of((block * BLK + c * HALF) % T, BLK), BLK)

    mine = rows_of(dout)
    own = [
        pltpu.make_async_copy(tok_hbm, tg.at[0, mine], lsem.at[0]),
        pltpu.make_async_copy(og_hbm, tg.at[1, mine], lsem.at[1]),
    ]
    for cp in own:
        cp.start()

    def weight_copies(i):
        cols = pl.ds(pl.multiple_of(i * C, 128), C)
        return [
            pltpu.make_async_copy(gw.at[:, cols], wgu.at[i, :, pl.ds(0, C)], gusem.at[i, 0]),
            pltpu.make_async_copy(uw.at[:, cols], wgu.at[i, :, pl.ds(C, C)], gusem.at[i, 1]),
            pltpu.make_async_copy(dw.at[cols], wd.at[i], dsem.at[i]),
        ]

    @pl.loop(0, N)
    def _(i):
        for cp in weight_copies(i):
            cp.start()

    barrier = pltpu.get_barrier_semaphore()

    def greet(dev):
        pl.semaphore_signal(barrier, inc=1, device_id=dev, device_id_type=MESH)

    for k in range(1, 8):
        greet((dp, (din + k) % 8, dout))
        greet((dp, din, (dout + k) % 8))
    for k in range(1, 4):
        greet(((dp + k) % 4, din, dout))
        greet(((dp + k) % 4, din, (dout + 4) % 8))

    def fill_mask(ref, values, start, rows):
        @pl.loop(0, rows // 64)
        def _(b):
            idx = lax.broadcasted_iota(jnp.int32, (64, 128), 0) + (b * 64 + start)
            hit = idx == values[0]
            for k in range(1, 16):
                hit = hit | (idx == values[k])
            ref[pl.ds(pl.multiple_of(b * 64, 64), 64), :] = jnp.where(hit, 1.0, 0.0)

    fill_mask(kin, oi, din * KB, KB)
    fill_mask(khid, oh, dout * HB, HB)
    for i in range(N):
        sgu[i, :, 0:C] = gs[:, i * C : (i + 1) * C]
        sgu[i, :, C:C2] = us[:, i * C : (i + 1) * C]
    igu[...] = 1.0 / (7.0 * sgu[...])
    idn[...] = 1.0 / (7.0 * ds[...])
    acc[...] = jnp.zeros_like(acc)
    dterm[...] = jnp.zeros_like(dterm)

    pl.semaphore_wait(barrier, 20)
    for cp in own:
        cp.wait()

    zcopy = remote(tg.at[:, mine], tg.at[:, mine], zs, zr, at_x(x, 1 - zh))
    zcopy.start()
    theirs = rows_of((dout + 4) % 8)

    def xcopy(which, k):
        rows = mine if which == 0 else theirs
        return remote(tg.at[:, rows], tg.at[:, rows], xs.at[which, k - 1], xr.at[which, k - 1], at_x(x + k, zh))

    def xarrive(which, k):
        rows = rows_of((x + 4 - k) % 4 + 4 * (zh if which == 0 else 1 - zh))
        return remote(tg.at[:, rows], tg.at[:, rows], xs.at[which, k - 1], xr.at[which, k - 1], at_x(x + k, zh))

    for k in (1, 3, 2):
        xcopy(0, k).start()

    def do_quant(i):
        for cp in weight_copies(i):
            cp.wait()
        for part in range(2):
            lanes = pl.ds(part * C, C)
            step, inv = sgu[i, :, lanes], igu[i, :, lanes]

            def body(b, carry):
                rows = pl.ds(pl.multiple_of(b * 64, 64), 64)
                keep = kin[rows, :][:, :1] > 0
                q, f = quant(wgu[i, rows, lanes], step, inv, keep)
                wgu[i, rows, lanes] = q
                fgu[i, rows, lanes] = f
                return carry

            lax.fori_loop(0, KB // 64, body, 0, unroll=2)
        for part in range(2):
            lanes = pl.ds(part * 512, 512)
            step, inv = ds[:, lanes], idn[:, lanes]

            def body(b, carry):
                rows = pl.ds(pl.multiple_of(b * 64, 64), 64)
                keep = khid[pl.ds(pl.multiple_of(i * C + b * 64, 64), 64), :][:, :1] > 0
                q, f = quant(wd[i, rows, lanes], step, inv, keep)
                wd[i, rows, lanes] = q
                fd[i, rows, lanes] = f
                return carry

            lax.fori_loop(0, C // 64, body, 0, unroll=2)

    def sib1(i):
        return remote(send1.at[i], recv1.at[i], s1s.at[i], s1r.at[i], sibling)

    def do_forward(i):
        for n in range(3):
            cols = slice(n * 256, (n + 1) * 256)
            z = dot(tg[0], wgu[i, :, cols])
            pre[i, :, cols] = z[:HALF]
            send1[i, :, cols] = z[HALF:].astype(BF)
        z = dot_t(tg[1], wd[i])
        pre[i, :, C2:] = z[:HALF]
        send1[i, :, C2:] = z[HALF:].astype(BF)
        sib1(i).start()

    def ycopy(i, k):
        rows = pl.ds(pl.multiple_of(((y + k) % 4) * BLK, BLK), BLK)
        return remote(send2.at[i, rows], recv2.at[i, k - 1], y2s.at[i, k - 1], y2r.at[i, k - 1], at_y(y + k, c))

    def do_pair_sum(i):
        sib1(i).wait_recv()
        total = pre[i] + recv1[i].astype(F32)
        pre[i] = total
        send2[i] = total.astype(BF)
        for k in (2, 1, 3):
            ycopy(i, k).start()

    myrow = pl.ds(pl.multiple_of(y * BLK, BLK), BLK)

    def agcopy(i, k):
        return remote(act.at[i, myrow], act.at[i, myrow], ags.at[i, k - 1], agr.at[i, k - 1], at_y(y + k, c))

    def agarrive(i, k):
        rows = pl.ds(pl.multiple_of(((y + 4 - k) % 4) * BLK, BLK), BLK)
        return remote(act.at[i, rows], act.at[i, rows], ags.at[i, k - 1], agr.at[i, k - 1], at_y(y + k, c))

    def do_act(i):
        for k in (1, 3, 2):
            ycopy(i, k).wait_recv()
        own_rows = pre[i, myrow]

        def summed(lo, hi):
            v = own_rows[:, lo:hi]
            for k in range(3):
                v = v + recv2[i, k, :, lo:hi].astype(F32)
            return v

        gate, up, back = summed(0, C), summed(C, C2), summed(C2, C3)
        p = jax.nn.sigmoid(gate)
        gp = gate * p
        act[i, myrow, 0:C] = (back * up * p * (1.0 + gate * (1.0 - p))).astype(BF)
        act[i, myrow, C:C2] = (back * gp).astype(BF)
        act[i, myrow, C2:C3] = (gp * up).astype(BF)
        for k in (2, 1, 3):
            agcopy(i, k).start()

    def sib2(i):
        return remote(
            act.at[i, pl.ds(0, HALF)], act.at[i, pl.ds(HALF, HALF)], s2s.at[i], s2r.at[i], sibling
        )

    def do_share(i):
        for k in (1, 3, 2):
            agarrive(i, k).wait_recv()
        sib2(i).start()

    def do_back(i):
        sib2(i).wait_recv()
        for n in range(4):
            cols = slice(n * 256, (n + 1) * 256)
            acc[:, cols] += dot_t(act[i, :, 0:C2], wgu[i, cols, :])
        for n in range(3):
            cols = slice(n * 256, (n + 1) * 256)
            z = dot(tg[0], fgu[i, :, cols])
            term = jnp.sum(act[i, :, cols].astype(F32) * z, axis=0, keepdims=True)
            gt[i, :, cols] = term
        for n in range(4):
            cols = slice(n * 256, (n + 1) * 256)
            z = dot(act[i, :, C2:C3], fd[i, :, cols])
            dterm[:, cols] += jnp.sum(tg[1, :, cols].astype(F32) * z, axis=0, keepdims=True)

    @pl.loop(0, N + 3)
    def _(i):
        @pl.when(i < N)
        def _():
            do_quant(i)

        @pl.when(i == 0)
        def _():
            zcopy.wait_recv()
            for k in (1, 3, 2):
                xcopy(1, k).start()

        @pl.when(i >= 3)
        def _():
            do_share(i - 3)

        @pl.when(i == 1)
        def _():
            for which in range(2):
                for k in range(1, 4):
                    xarrive(which, k).wait_recv()

        @pl.when((i >= 1) & (i < N + 1))
        def _():
            do_forward(i - 1)

        @pl.when((i >= 2) & (i < N + 2))
        def _():
            do_act(i - 2)

        @pl.when((i >= 1) & (i < N + 1))
        def _():
            do_pair_sum(i - 1)

        @pl.when(i >= 3)
        def _():
            do_back(i - 3)

    esend[...] = acc[...].astype(BF)

    def ecopy(k):
        return remote(
            esend.at[rows_of((dout + k) % 8)], erecv.at[k - 1], es.at[k - 1], er.at[k - 1],
            (dp, din, (dout + k) % 8),
        )

    for k in (4, 3, 5, 2, 6, 1, 7):
        ecopy(k).start()

    gslot[din] = gt[...]
    dslot[x] = dterm[...]

    def gcopy(k):
        return remote(gt, gslot.at[din], gs_s.at[k - 1], gs_r.at[din], (dp, (din + k) % 8, dout))

    def garrive(k):
        src = (din + k) % 8
        return remote(gt, gslot.at[src], gs_s.at[k - 1], gs_r.at[src], (dp, src, dout))

    def dcopy(k):
        return remote(dterm, dslot.at[x], ds_s.at[k - 1], ds_r.at[x], at_x(x + k, zh))

    def darrive(k):
        src = (x + k) % 4
        return remote(dterm, dslot.at[src], ds_s.at[k - 1], ds_r.at[src], at_x(src, zh))

    for k in range(1, 4):
        dcopy(k).start()
    for k in range(1, 8):
        gcopy(k).start()
    for k in range(1, 4):
        darrive(k).wait_recv()
    part = dslot[0]
    for k in range(1, 4):
        part = part + dslot[k]
    zi = zh * 4 + dp
    dz[zi] = part

    def at_z(k):
        return (k % 4, din, (k // 4) * 4 + x)

    def zzcopy(k):
        return remote(dz.at[zi], dz.at[zi], dz_s.at[k - 1], dz_r.at[zi], at_z((zi + k) % 8))

    def zzarrive(k):
        src = (zi + k) % 8
        return remote(dz.at[src], dz.at[src], dz_s.at[k - 1], dz_r.at[src], at_z(src))

    for k in range(1, 8):
        zzcopy(k).start()
    for k in range(1, 8):
        garrive(k).wait_recv()
    part = gslot[0]
    for k in range(1, 8):
        part = part + gslot[k]
    gdp[dp] = part

    def gpcopy(k):
        return remote(gdp.at[dp], gdp.at[dp], gp_s.at[k - 1], gp_r.at[dp], ((dp + k) % 4, din, dout))

    def gparrive(k):
        src = (dp + k) % 4
        return remote(gdp.at[src], gdp.at[src], gp_s.at[k - 1], gp_r.at[src], (src, din, dout))

    for k in range(1, 4):
        gpcopy(k).start()
    for k in range(1, 8):
        ecopy(k).wait_recv()
    total = acc[rows_of(dout), :]
    for k in range(7):
        total = total + erecv[k].astype(F32)
    dt_out[...] = total.astype(BF)
    for k in range(1, 4):
        gparrive(k).wait_recv()
    part = gdp[0]
    for k in range(1, 4):
        part = part + gdp[k]
    part = part * SCALE_IN
    for i in range(N):
        gg_out[:, i * C : (i + 1) * C] = part[i, :, 0:C]
        ug_out[:, i * C : (i + 1) * C] = part[i, :, C:C2]
    for k in range(1, 8):
        zzarrive(k).wait_recv()
    part = dz[0]
    for k in range(1, 8):
        part = part + dz[k]
    dg_out[...] = part * SCALE_HID

    zcopy.wait_send()
    for k in range(1, 4):
        for which in range(2):
            xcopy(which, k).wait_send()
        dcopy(k).wait_send()
        gpcopy(k).wait_send()
    for k in range(1, 8):
        ecopy(k).wait_send()
        gcopy(k).wait_send()
        zzcopy(k).wait_send()

    @pl.loop(0, N)
    def _(i):
        sib1(i).wait_send()
        sib2(i).wait_send()
        for k in range(1, 4):
            ycopy(i, k).wait_send()
            agcopy(i, k).wait_send()


def shards(tokens, out_grad, gate_weight, up_weight, down_weight, gate_step, up_step, down_step, outlier_in, outlier_hidden):
    hbm = pl.BlockSpec(memory_space=pl.ANY)
    vmem = pl.BlockSpec(memory_space=pltpu.VMEM)
    smem = pl.BlockSpec(memory_space=pltpu.SMEM)
    V, S = pltpu.VMEM, pltpu.SemaphoreType.DMA
    d_tokens, gg, ug, dg = pl.pallas_call(
        kernel,
        out_shape=(
            jax.ShapeDtypeStruct((BLK, KB), BF),
            jax.ShapeDtypeStruct((1, HB), F32),
            jax.ShapeDtypeStruct((1, HB), F32),
            jax.ShapeDtypeStruct((1, KB), F32),
        ),
        in_specs=[hbm, hbm, hbm, hbm, hbm, vmem, vmem, vmem, smem, smem],
        out_specs=(vmem, vmem, vmem, vmem),
        scratch_shapes=[
            V((2, T, KB), BF),
            V((N, KB, C2), BF),
            V((N, KB, C2), BF),
            V((N, C, KB), BF),
            V((N, C, KB), BF),
            V((KB, 128), F32),
            V((HB, 128), F32),
            V((N, 1, C2), F32),
            V((N, 1, C2), F32),
            V((1, KB), F32),
            V((N, HALF, C3), F32),
            V((N, HALF, C3), BF),
            V((N, HALF, C3), BF),
            V((N, HALF, C3), BF),
            V((N, 3, BLK, C3), BF),
            V((N, T, C3), BF),
            V((T, KB), F32),
            V((T, KB), BF),
            V((7, BLK, KB), BF),
            V((N, 1, C2), F32),
            V((8, N, 1, C2), F32),
            V((4, N, 1, C2), F32),
            V((1, KB), F32),
            V((4, 1, KB), F32),
            V((8, 1, KB), F32),
            S((2,)),
            S((N, 2)),
            S((N,)),
            S, S,
            S((2, 3)), S((2, 3)),
            S((N,)), S((N,)),
            S((N, 3)), S((N, 3)),
            S((N, 3)), S((N, 3)),
            S((N,)), S((N,)),
            S((7,)), S((7,)),
            S((7,)), S((8,)),
            S((3,)), S((4,)),
            S((3,)), S((4,)),
            S((7,)), S((8,)),
        ],
        compiler_params=pltpu.CompilerParams(
            collective_id=0, has_side_effects=True, vmem_limit_bytes=56 * 2**20
        ),
        name="swiglu_back",
    )(
        tokens, out_grad, gate_weight, up_weight, down_weight,
        gate_step.reshape(1, HB), up_step.reshape(1, HB), down_step.reshape(1, KB),
        outlier_in, outlier_hidden,
    )
    return d_tokens, gg.reshape(HB), ug.reshape(HB), dg.reshape(KB)


def solution(mesh):
    return jax.shard_map(
        shards,
        mesh=mesh,
        in_specs=(
            P(("dp", "dout"), "din"),
            P(("dp", "dout"), "din"),
            P("din", "dout"),
            P("din", "dout"),
            P("dout", "din"),
            P("dout"),
            P("dout"),
            P("din"),
            P("din"),
            P("dout"),
        ),
        out_specs=(P(("dp", "dout"), "din"), P("dout"), P("dout"), P("din")),
        check_vma=False,
    )
```

```python
import math

import jax
import jax.numpy as jnp
from jax import lax
from jax.experimental import pallas as pl
from jax.experimental.pallas import tpu as pltpu
from jax.sharding import PartitionSpec as P

D = 8192
FF = 15360
TOK_DEV = 256
SCALE_IN = 1.0 / math.sqrt(D * TOK_DEV)
SCALE_HID = 1.0 / math.sqrt(FF * TOK_DEV)

KB = 1024
HB = 1920
N = 5
C = HB // N
C2, C3 = 2 * C, 3 * C
T = 256
HALF = T // 2
BLK = 32

MESH = pl.DeviceIdType.MESH
BF, F32 = jnp.bfloat16, jnp.float32

SIN = (3.14158202, -5.16714276, 2.5418987, -0.55463534)


def quant(w, step, inv7, keep):
    w = w.astype(F32)
    x = w * inv7
    t = jnp.tanh(x)
    c = 7.0 * t
    r = c - jnp.round(c)
    u = r * r
    p = jnp.float32(SIN[3])
    for k in (2, 1, 0):
        p = p * u + jnp.float32(SIN[k])
    sn = p * r
    s2 = sn * sn
    d = jnp.maximum(1.0 - s2, 1e-12)
    cs = d * lax.rsqrt(d)
    shaped = c - sn * cs * jnp.float32(0.9 / math.pi)
    slope7 = (0.7 + 12.6 * s2) * (1.0 - t * t)
    q = jnp.where(keep, w, step * shaped)
    f = jnp.where(keep, 0.0, shaped - x * slope7)
    return q.astype(BF), f.astype(BF)


def remote(src, dst, ssem, rsem, dev):
    return pltpu.make_async_remote_copy(
        src_ref=src, dst_ref=dst, send_sem=ssem, recv_sem=rsem, device_id=dev, device_id_type=MESH
    )


def dot(a, b):
    return jnp.dot(a, b, preferred_element_type=F32)


def dot_t(a, b):
    return lax.dot_general(a, b, (((1,), (1,)), ((), ())), preferred_element_type=F32)


def kernel(
    tok_hbm, og_hbm, gw, uw, dw, gs, us, ds, oi, oh,
    dt_out, gu_out, dg_out,
    tg, wgu, fgu, wd, fd, kin, khid, sgu, igu, sdn, idn,
    pre, send1, recv1, send2, recv2, act,
    acc, esend, erecv, ezsend, ezrecv, gt, gslot, gdp, dterm, dslot, dz,
    lsem, gusem, dsem, zs, zr, xs, xr, s1s, s1r, y2s, y2r, ags, agr, s2s, s2r,
    es, er, ezs, ezr, gs_s, gs_r, gp_s, gp_r, ds_s, ds_r, dz_s, dz_r,
):
    dp = lax.axis_index("dp")
    din = lax.axis_index("din")
    dout = lax.axis_index("dout")
    y, c = din // 2, din % 2
    zh, x = dout // 4, dout % 4

    def at_y(k, core):
        return (dp, (k % 4) * 2 + core, dout)

    def at_x(k, hi):
        return (dp, din, hi * 4 + k % 4)

    sibling = (dp, y * 2 + (1 - c), dout)

    def rows_of(block):
        return pl.ds(pl.multiple_of((block * BLK + c * HALF) % T, BLK), BLK)

    mine = rows_of(dout)
    own = [
        pltpu.make_async_copy(tok_hbm, tg.at[0, mine], lsem.at[0]),
        pltpu.make_async_copy(og_hbm, tg.at[1, mine], lsem.at[1]),
    ]
    for cp in own:
        cp.start()

    def weight_copies(i):
        cols = pl.ds(pl.multiple_of(i * C, 128), C)
        return [
            pltpu.make_async_copy(gw.at[:, cols], wgu.at[i, :, pl.ds(0, C)], gusem.at[i, 0]),
            pltpu.make_async_copy(uw.at[:, cols], wgu.at[i, :, pl.ds(C, C)], gusem.at[i, 1]),
        ]

    def down_copy(i):
        rows = pl.ds(pl.multiple_of(i * C, 128), C)
        return pltpu.make_async_copy(dw.at[rows], wd.at[i], dsem.at[i])

    @pl.loop(0, N)
    def _(i):
        for cp in weight_copies(i):
            cp.start()
        down_copy(i).start()

    barrier = pltpu.get_barrier_semaphore()

    def greet(dev):
        pl.semaphore_signal(barrier, inc=1, device_id=dev, device_id_type=MESH)

    for k in range(1, 8):
        greet((dp, (din + k) % 8, dout))
        greet((dp, din, (dout + k) % 8))
    for k in range(1, 4):
        greet(((dp + k) % 4, din, dout))
        greet(((dp + k) % 4, din, (dout + 4) % 8))

    def fill_mask(ref, values, start, rows):
        @pl.loop(0, rows // 64)
        def _(b):
            idx = lax.broadcasted_iota(jnp.int32, (64, 128), 0) + (b * 64 + start)
            hit = idx == values[0]
            for k in range(1, 16):
                hit = hit | (idx == values[k])
            ref[pl.ds(pl.multiple_of(b * 64, 64), 64), :] = jnp.where(hit, 1.0, 0.0)

    fill_mask(kin, oi, din * KB, KB)
    fill_mask(khid, oh, dout * HB, HB)
    for i in range(N):
        sgu[i, :, 0:C] = gs[i * C : (i + 1) * C].reshape(1, C)
        sgu[i, :, C:C2] = us[i * C : (i + 1) * C].reshape(1, C)
    sdn[...] = ds[...].reshape(1, KB)
    igu[...] = 1.0 / (7.0 * sgu[...])
    idn[...] = 1.0 / (7.0 * sdn[...])
    acc[...] = jnp.zeros_like(acc)
    dterm[...] = jnp.zeros_like(dterm)

    pl.semaphore_wait(barrier, 20)
    for cp in own:
        cp.wait()

    zcopy = remote(tg.at[:, mine], tg.at[:, mine], zs, zr, at_x(x, 1 - zh))
    zcopy.start()
    theirs = rows_of((dout + 4) % 8)

    def xcopy(which, k):
        rows = mine if which == 0 else theirs
        return remote(tg.at[:, rows], tg.at[:, rows], xs.at[which, k - 1], xr.at[which, k - 1], at_x(x + k, zh))

    def xarrive(which, k):
        rows = rows_of((x + 4 - k) % 4 + 4 * (zh if which == 0 else 1 - zh))
        return remote(tg.at[:, rows], tg.at[:, rows], xs.at[which, k - 1], xr.at[which, k - 1], at_x(x + k, zh))

    for k in (1, 3, 2):
        xcopy(0, k).start()

    def quant_rows(w_ref, f_ref, i, keep_ref, keep_at, rows, width, step_of, inv_of):
        def body(b, carry):
            at = pl.ds(pl.multiple_of(b * 128, 128), 128)
            keep = keep_ref[pl.ds(pl.multiple_of(keep_at + b * 128, 128), 128), :] > 0
            for strip in range(width // 128):
                lanes = pl.ds(strip * 128, 128)
                q, f = quant(w_ref[i, at, lanes], step_of(lanes), inv_of(lanes), keep)
                w_ref[i, at, lanes] = q
                f_ref[i, at, lanes] = f
            return carry

        lax.fori_loop(0, rows // 128, body, 0)

    def quant_gate_up(i):
        for cp in weight_copies(i):
            cp.wait()
        quant_rows(wgu, fgu, i, kin, 0, KB, C2, lambda l: sgu[i, :, l], lambda l: igu[i, :, l])

    def quant_down(i):
        down_copy(i).wait()
        quant_rows(wd, fd, i, khid, i * C, C, KB, lambda l: sdn[:, l], lambda l: idn[:, l])

    def sib1(i):
        return remote(send1.at[i], recv1.at[i], s1s.at[i], s1r.at[i], sibling)

    def do_forward(i):
        for n in range(3):
            cols = slice(n * 256, (n + 1) * 256)
            z = dot(tg[0], wgu[i, :, cols])
            pre[i, :, cols] = z[:HALF]
            send1[i, :, cols] = z[HALF:].astype(BF)
        z = dot_t(tg[1], wd[i])
        pre[i, :, C2:] = z[:HALF]
        send1[i, :, C2:] = z[HALF:].astype(BF)
        sib1(i).start()

    def ycopy(i, k):
        rows = pl.ds(pl.multiple_of(((y + k) % 4) * BLK, BLK), BLK)
        return remote(send2.at[i, rows], recv2.at[i, k - 1], y2s.at[i, k - 1], y2r.at[i, k - 1], at_y(y + k, c))

    def do_pair_sum(i):
        sib1(i).wait_recv()

        @pl.loop(0, HALF // BLK)
        def _(b):
            rows = pl.ds(pl.multiple_of(b * BLK, BLK), BLK)
            total = pre[i, rows, :] + recv1[i, rows, :].astype(F32)
            pre[i, rows, :] = total
            send2[i, rows, :] = total.astype(BF)

        for k in (2, 1, 3):
            ycopy(i, k).start()

    myrow = pl.ds(pl.multiple_of(y * BLK, BLK), BLK)

    def agcopy(i, k):
        return remote(act.at[i, myrow], act.at[i, myrow], ags.at[i, k - 1], agr.at[i, k - 1], at_y(y + k, c))

    def agarrive(i, k):
        rows = pl.ds(pl.multiple_of(((y + 4 - k) % 4) * BLK, BLK), BLK)
        return remote(act.at[i, rows], act.at[i, rows], ags.at[i, k - 1], agr.at[i, k - 1], at_y(y + k, c))

    def do_act(i):
        for k in (1, 3, 2):
            ycopy(i, k).wait_recv()
        own_rows = pre[i, myrow]

        def summed(lo, hi):
            v = own_rows[:, lo:hi]
            for k in range(3):
                v = v + recv2[i, k, :, lo:hi].astype(F32)
            return v

        gate, up, back = summed(0, C), summed(C, C2), summed(C2, C3)
        p = jax.nn.sigmoid(gate)
        gp = gate * p
        act[i, myrow, 0:C] = (back * up * p * (1.0 + gate * (1.0 - p))).astype(BF)
        act[i, myrow, C:C2] = (back * gp).astype(BF)
        act[i, myrow, C2:C3] = (gp * up).astype(BF)
        for k in (2, 1, 3):
            agcopy(i, k).start()

    def sib2(i):
        return remote(
            act.at[i, pl.ds(0, HALF)], act.at[i, pl.ds(HALF, HALF)], s2s.at[i], s2r.at[i], sibling
        )

    def do_share(i):
        for k in (1, 3, 2):
            agarrive(i, k).wait_recv()
        sib2(i).start()

    def do_d_tokens(i):
        sib2(i).wait_recv()
        for n in range(4):
            cols = slice(n * 256, (n + 1) * 256)
            acc[:, cols] += dot_t(act[i, :, 0:C2], wgu[i, cols, :])

    def do_terms(i):
        for n in range(3):
            cols = slice(n * 256, (n + 1) * 256)
            z = dot(tg[0], fgu[i, :, cols])
            term = jnp.sum(act[i, :, cols].astype(F32) * z, axis=0, keepdims=True)
            gt[i, :, cols] = term
        for n in range(4):
            cols = slice(n * 256, (n + 1) * 256)
            z = dot(act[i, :, C2:C3], fd[i, :, cols])
            dterm[:, cols] += jnp.sum(tg[1, :, cols].astype(F32) * z, axis=0, keepdims=True)

    def ecopy(part, k):
        hi = 1 - zh if part == 0 else zh
        return remote(
            esend.at[rows_of(hi * 4 + (x + k) % 4)], erecv.at[part, k - 1],
            es.at[part, k - 1], er.at[part, k - 1], at_x(x + k, zh),
        )

    ezcopy = remote(ezsend, ezrecv, ezs, ezr, at_x(x, 1 - zh))

    def start_d_tokens():
        for part in range(2):
            for k in (2, 1, 3):
                rows = rows_of((1 - zh if part == 0 else zh) * 4 + (x + k) % 4)
                esend[rows, :] = acc[rows, :].astype(BF)
                ecopy(part, k).start()

    @pl.loop(0, N)
    def _(i):
        quant_gate_up(i)

        @pl.when(i == 1)
        def _():
            zcopy.wait_recv()
            for k in (1, 3, 2):
                xcopy(1, k).start()

        @pl.when(i == 3)
        def _():
            do_pair_sum(2)

        @pl.when(i >= 3)
        def _():
            do_act((i - 3) * 2)

        quant_down(i)

        @pl.when(i == 2)
        def _():
            for which in range(2):
                for k in range(1, 4):
                    xarrive(which, k).wait_recv()

        first = jnp.where(i == 2, 0, i)
        last = jnp.where(i < 2, i, i + 1)

        @pl.loop(first, last)
        def _(m):
            do_forward(m)

            @pl.when((i == 2) & (m >= 1))
            def _():
                do_pair_sum(m - 1)

        @pl.when(i == 3)
        def _():
            do_act(1)

        @pl.when(i == 4)
        def _():
            do_share(0)

        @pl.when(i >= 3)
        def _():
            do_pair_sum(i)

    @pl.loop(0, N)
    def _(i):
        @pl.when(i == 0)
        def _():
            do_share(1)
            do_act(3)

        @pl.when(i == 2)
        def _():
            do_act(4)

        @pl.when(i >= 3)
        def _():
            do_share(i)

        do_d_tokens(i)

        @pl.when(i == N - 1)
        def _():
            start_d_tokens()

        do_terms(i)

        @pl.when(i == 1)
        def _():
            do_share(2)

    gslot[din] = gt[...]
    dslot[x] = dterm[...]

    def gcopy(k):
        return remote(gt, gslot.at[din], gs_s.at[k - 1], gs_r.at[din], (dp, (din + k) % 8, dout))

    def garrive(k):
        src = (din + k) % 8
        return remote(gt, gslot.at[src], gs_s.at[k - 1], gs_r.at[src], (dp, src, dout))

    def dcopy(k):
        return remote(dterm, dslot.at[x], ds_s.at[k - 1], ds_r.at[x], at_x(x + k, zh))

    def darrive(k):
        src = (x + k) % 4
        return remote(dterm, dslot.at[src], ds_s.at[k - 1], ds_r.at[src], at_x(src, zh))

    for k in range(1, 4):
        dcopy(k).start()
    for k in range(1, 8):
        gcopy(k).start()
    for k in range(1, 4):
        ecopy(0, k).wait_recv()
    total = acc[rows_of((dout + 4) % 8), :]
    for k in range(3):
        total = total + erecv[0, k].astype(F32)
    ezsend[...] = total.astype(BF)
    ezcopy.start()
    for k in range(1, 4):
        darrive(k).wait_recv()
    part = dslot[0]
    for k in range(1, 4):
        part = part + dslot[k]
    zi = zh * 4 + dp
    dz[zi] = part

    def at_z(k):
        return (k % 4, din, (k // 4) * 4 + x)

    def zzcopy(k):
        return remote(dz.at[zi], dz.at[zi], dz_s.at[k - 1], dz_r.at[zi], at_z((zi + k) % 8))

    def zzarrive(k):
        src = (zi + k) % 8
        return remote(dz.at[src], dz.at[src], dz_s.at[k - 1], dz_r.at[src], at_z(src))

    for k in range(1, 8):
        zzcopy(k).start()
    for k in range(1, 8):
        garrive(k).wait_recv()
    part = gslot[0]
    for k in range(1, 8):
        part = part + gslot[k]
    gdp[dp] = part

    def gpcopy(k):
        return remote(gdp.at[dp], gdp.at[dp], gp_s.at[k - 1], gp_r.at[dp], ((dp + k) % 4, din, dout))

    def gparrive(k):
        src = (dp + k) % 4
        return remote(gdp.at[src], gdp.at[src], gp_s.at[k - 1], gp_r.at[src], (src, din, dout))

    for k in range(1, 4):
        gpcopy(k).start()
    for k in range(1, 4):
        ecopy(1, k).wait_recv()
    total = acc[rows_of(dout), :]
    for k in range(3):
        total = total + erecv[1, k].astype(F32)
    ezcopy.wait_recv()
    dt_out[...] = (total + ezrecv[...].astype(F32)).astype(BF)
    for k in range(1, 4):
        gparrive(k).wait_recv()
    part = gdp[0]
    for k in range(1, 4):
        part = part + gdp[k]
    gu_out[...] = part * SCALE_IN
    for k in range(1, 8):
        zzarrive(k).wait_recv()
    part = dz[0]
    for k in range(1, 8):
        part = part + dz[k]
    dg_out[...] = part * SCALE_HID

    zcopy.wait_send()
    ezcopy.wait_send()
    for k in range(1, 4):
        for which in range(2):
            xcopy(which, k).wait_send()
            ecopy(which, k).wait_send()
        dcopy(k).wait_send()
        gpcopy(k).wait_send()
    for k in range(1, 8):
        gcopy(k).wait_send()
        zzcopy(k).wait_send()

    @pl.loop(0, N)
    def _(i):
        sib1(i).wait_send()
        sib2(i).wait_send()
        for k in range(1, 4):
            ycopy(i, k).wait_send()
            agcopy(i, k).wait_send()


def place(dt, gu, dg, dt_out, gg_out, ug_out, dg_out):
    dt_out[...] = dt[...]
    for i in range(N):
        gg_out[i * C : (i + 1) * C] = gu[i, :, 0:C].reshape(C)
        ug_out[i * C : (i + 1) * C] = gu[i, :, C:C2].reshape(C)
    dg_out[...] = dg[...].reshape(KB)


def shards(tokens, out_grad, gate_weight, up_weight, down_weight, gate_step, up_step, down_step, outlier_in, outlier_hidden):
    hbm = pl.BlockSpec(memory_space=pl.ANY)
    vmem = pl.BlockSpec(memory_space=pltpu.VMEM)
    smem = pl.BlockSpec(memory_space=pltpu.SMEM)
    V, S = pltpu.VMEM, pltpu.SemaphoreType.DMA
    results = pl.pallas_call(
        kernel,
        out_shape=(
            jax.ShapeDtypeStruct((BLK, KB), BF),
            jax.ShapeDtypeStruct((N, 1, C2), F32),
            jax.ShapeDtypeStruct((1, KB), F32),
        ),
        in_specs=[hbm, hbm, hbm, hbm, hbm, vmem, vmem, vmem, smem, smem],
        out_specs=(vmem, vmem, vmem),
        scratch_shapes=[
            V((2, T, KB), BF),
            V((N, KB, C2), BF),
            V((N, KB, C2), BF),
            V((N, C, KB), BF),
            V((N, C, KB), BF),
            V((KB, 128), F32),
            V((HB, 128), F32),
            V((N, 1, C2), F32),
            V((N, 1, C2), F32),
            V((1, KB), F32),
            V((1, KB), F32),
            V((N, HALF, C3), F32),
            V((N, HALF, C3), BF),
            V((N, HALF, C3), BF),
            V((N, HALF, C3), BF),
            V((N, 3, BLK, C3), BF),
            V((N, T, C3), BF),
            V((T, KB), F32),
            V((T, KB), BF),
            V((2, 3, BLK, KB), BF),
            V((BLK, KB), BF),
            V((BLK, KB), BF),
            V((N, 1, C2), F32),
            V((8, N, 1, C2), F32),
            V((4, N, 1, C2), F32),
            V((1, KB), F32),
            V((4, 1, KB), F32),
            V((8, 1, KB), F32),
            S((2,)),
            S((N, 2)),
            S((N,)),
            S, S,
            S((2, 3)), S((2, 3)),
            S((N,)), S((N,)),
            S((N, 3)), S((N, 3)),
            S((N, 3)), S((N, 3)),
            S((N,)), S((N,)),
            S((2, 3)), S((2, 3)),
            S, S,
            S((7,)), S((8,)),
            S((3,)), S((4,)),
            S((3,)), S((4,)),
            S((7,)), S((8,)),
        ],
        compiler_params=pltpu.CompilerParams(
            collective_id=0, has_side_effects=True, vmem_limit_bytes=56 * 2**20
        ),
        name="swiglu_back",
    )(
        tokens, out_grad, gate_weight, up_weight, down_weight,
        gate_step, up_step, down_step,
        outlier_in, outlier_hidden,
    )
    return pl.pallas_call(
        place,
        out_shape=(
            jax.ShapeDtypeStruct((BLK, KB), BF),
            jax.ShapeDtypeStruct((HB,), F32),
            jax.ShapeDtypeStruct((HB,), F32),
            jax.ShapeDtypeStruct((KB,), F32),
        ),
        in_specs=[vmem] * 3,
        out_specs=(vmem,) * 4,
        name="place",
    )(*results)


def solution(mesh):
    return jax.shard_map(
        shards,
        mesh=mesh,
        in_specs=(
            P(("dp", "dout"), "din"),
            P(("dp", "dout"), "din"),
            P("din", "dout"),
            P("din", "dout"),
            P("dout", "din"),
            P("dout"),
            P("dout"),
            P("din"),
            P("din"),
            P("dout"),
        ),
        out_specs=(P(("dp", "dout"), "din"), P("dout"), P("dout"), P("din")),
        check_vma=False,
    )
```

```python
import math

import jax
import jax.numpy as jnp
from jax import lax
from jax.experimental import pallas as pl
from jax.experimental.pallas import tpu as pltpu
from jax.sharding import PartitionSpec as P

D = 8192
FF = 15360
TOK_DEV = 256
SCALE_IN = 1.0 / math.sqrt(D * TOK_DEV)
SCALE_HID = 1.0 / math.sqrt(FF * TOK_DEV)

KB = 1024
HB = 1920
N = 5
C = HB // N
C2, C3 = 2 * C, 3 * C
T = 256
HALF = T // 2
BLK = 32
QTR = 64
SUB = 16
SPLIT = 3

MESH = pl.DeviceIdType.MESH
BF, F32 = jnp.bfloat16, jnp.float32

SIN = (3.14158202, -5.16714276, 2.5418987, -0.55463534)


def quant(w, step, inv7, keep):
    w = w.astype(F32)
    x = w * inv7
    t = jnp.tanh(x)
    c = 7.0 * t
    r = c - jnp.round(c)
    u = r * r
    p = jnp.float32(SIN[3])
    for k in (2, 1, 0):
        p = p * u + jnp.float32(SIN[k])
    sn = p * r
    s2 = sn * sn
    d = jnp.maximum(1.0 - s2, 1e-12)
    cs = d * lax.rsqrt(d)
    shaped = c - sn * cs * jnp.float32(0.9 / math.pi)
    slope7 = (0.7 + 12.6 * s2) * (1.0 - t * t)
    q = jnp.where(keep, w, step * shaped)
    f = jnp.where(keep, 0.0, shaped - x * slope7)
    return q.astype(BF), f.astype(BF)


def remote(src, dst, ssem, rsem, dev):
    return pltpu.make_async_remote_copy(
        src_ref=src, dst_ref=dst, send_sem=ssem, recv_sem=rsem, device_id=dev, device_id_type=MESH
    )


def dot(a, b):
    return jnp.dot(a, b, preferred_element_type=F32)


def dot_t(a, b):
    return lax.dot_general(a, b, (((1,), (1,)), ((), ())), preferred_element_type=F32)


def kernel(
    tok_hbm, og_hbm, gw, uw, dw, gs, us, ds, oi, oh,
    dt_out, gu_out, dg_out,
    tg, wgu, fgu, wd, fd, kin, khid, sgu, igu, sdn, idn,
    pre, send1, recv1, send2, recv2, act,
    acc, esend, erecv, ezsend, ezrecv, gt, gslot, gdp, dterm, dslot, dz,
    lsem, gusem, dsem, zs, zr, xs, xr, s1s, s1r, y2s, y2r, ags, agr, s2s, s2r,
    es, er, ezs, ezr, gs_s, gs_r, gp_s, gp_r, ds_s, ds_r, dz_s, dz_r,
):
    dp = lax.axis_index("dp")
    din = lax.axis_index("din")
    dout = lax.axis_index("dout")
    y, c = din // 2, din % 2
    zh, x = dout // 4, dout % 4

    def at_y(k, core):
        return (dp, (k % 4) * 2 + core, dout)

    def at_x(k, hi):
        return (dp, din, hi * 4 + k % 4)

    sibling = (dp, y * 2 + (1 - c), dout)

    def rows_of(side, k):
        return pl.ds(pl.multiple_of(side * HALF + ((k % 4) * BLK + c * QTR) % HALF, BLK), BLK)

    barrier = pltpu.get_barrier_semaphore()

    def greet(dev):
        pl.semaphore_signal(barrier, inc=1, device_id=dev, device_id_type=MESH)

    for k in range(1, 8):
        greet((dp, (din + k) % 8, dout))
        greet((dp, din, (dout + k) % 8))
    for k in range(1, 4):
        greet(((dp + k) % 4, din, dout))
        greet(((dp + k) % 4, din, (dout + 4) % 8))

    mine = rows_of(0, x)
    own = [
        pltpu.make_async_copy(tok_hbm, tg.at[0, mine], lsem.at[0]),
        pltpu.make_async_copy(og_hbm, tg.at[1, mine], lsem.at[1]),
    ]
    for cp in own:
        cp.start()

    def weight_copies(i):
        cols = pl.ds(pl.multiple_of(i * C, 128), C)
        return [
            pltpu.make_async_copy(gw.at[:, cols], wgu.at[i, :, pl.ds(0, C)], gusem.at[i, 0]),
            pltpu.make_async_copy(uw.at[:, cols], wgu.at[i, :, pl.ds(C, C)], gusem.at[i, 1]),
        ]

    def down_copy(i):
        rows = pl.ds(pl.multiple_of(i * C, 128), C)
        return pltpu.make_async_copy(dw.at[rows], wd.at[i], dsem.at[i])

    @pl.loop(0, N)
    def _(i):
        for cp in weight_copies(i):
            cp.start()
        down_copy(i).start()

    def fill_mask(ref, values, start, rows, block):
        lane = lax.broadcasted_iota(jnp.int32, (block, 128), 1)
        row = lax.broadcasted_iota(jnp.int32, (block, 128), 0)
        listed = jnp.full((1, 128), -1, jnp.int32)
        for k in range(16):
            listed = jnp.where(lane[:1] == k, values[k] - start, listed)
        ones = jnp.ones((128, 128), BF)

        @pl.loop(0, rows // block)
        def _(b):
            hit = jnp.where(row + b * block == listed, 1.0, 0.0).astype(BF)
            ref[pl.ds(pl.multiple_of(b * block, block), block), :] = dot(hit, ones)

    fill_mask(kin, oi, din * KB, KB, 256)
    fill_mask(khid, oh, dout * HB, HB, 384)
    acc[...] = jnp.zeros_like(acc)
    for i in range(N):
        sgu[i, :, 0:C] = gs[i * C : (i + 1) * C].reshape(1, C)
        sgu[i, :, C:C2] = us[i * C : (i + 1) * C].reshape(1, C)
    sdn[...] = ds[...].reshape(1, KB)
    igu[...] = 1.0 / (7.0 * sgu[...])
    idn[...] = 1.0 / (7.0 * sdn[...])
    dterm[...] = jnp.zeros_like(dterm)

    theirs = rows_of(1, x)
    zcopy = remote(tg.at[:, mine], tg.at[:, theirs], zs, zr, at_x(x, 1 - zh))

    def xcopy(which, k):
        rows = mine if which == 0 else theirs
        return remote(tg.at[:, rows], tg.at[:, rows], xs.at[which, k - 1], xr.at[which, k - 1], at_x(x + k, zh))

    def xarrive(which, k):
        rows = rows_of(which, x + 4 - k)
        return remote(tg.at[:, rows], tg.at[:, rows], xs.at[which, k - 1], xr.at[which, k - 1], at_x(x + k, zh))

    def start_gather():
        pl.semaphore_wait(barrier, 20)
        for cp in own:
            cp.wait()
        zcopy.start()
        for k in (1, 3, 2):
            xcopy(0, k).start()

    def pass_gather():
        zcopy.wait_recv()
        for k in (1, 3, 2):
            xcopy(1, k).start()

    def wait_gather(which):
        for k in (1, 3, 2):
            xarrive(which, k).wait_recv()

    def quant_rows(w_ref, f_ref, i, keep_ref, keep_at, lo, hi, width, step_of, inv_of):
        def body(b, carry):
            at = pl.ds(pl.multiple_of(b * 128, 128), 128)
            keep = keep_ref[pl.ds(pl.multiple_of(keep_at + b * 128, 128), 128), :] > 0
            for strip in range(width // 128):
                lanes = pl.ds(strip * 128, 128)
                q, f = quant(w_ref[i, at, lanes], step_of(lanes), inv_of(lanes), keep)
                w_ref[i, at, lanes] = q
                f_ref[i, at, lanes] = f
            return carry

        lax.fori_loop(lo // 128, hi // 128, body, 0)

    def quant_gate_up(i, lo, hi):
        if lo == 0:
            for cp in weight_copies(i):
                cp.wait()
        quant_rows(wgu, fgu, i, kin, 0, lo, hi, C2, lambda l: sgu[i, :, l], lambda l: igu[i, :, l])

    def quant_down(i):
        down_copy(i).wait()
        quant_rows(wd, fd, i, khid, i * C, 0, C, KB, lambda l: sdn[:, l], lambda l: idn[:, l])

    def sib1(i, u, n):
        sides = pl.ds(u, n)
        return remote(send1.at[i, sides], recv1.at[i, sides], s1s.at[i, u], s1r.at[i, u], sibling)

    def do_forward(i, u, n):
        def put(z, cols):
            for v in range(n):
                pre[i, u + v, :, cols] = z[v * HALF : v * HALF + QTR]
                send1[i, u + v, :, cols] = z[v * HALF + QTR : (v + 1) * HALF].astype(BF)

        tokens = slice(u * HALF, (u + n) * HALF)
        for k in range(3):
            cols = slice(k * 256, (k + 1) * 256)
            put(dot(tg[0, tokens], wgu[i, :, cols]), cols)
        put(dot_t(tg[1, tokens], wd[i]), slice(C2, C3))
        sib1(i, u, n).start()

    def ycopy(i, u, n, k):
        sides = pl.ds(u, n)
        rows = pl.ds(pl.multiple_of(((y + k) % 4) * SUB, SUB), SUB)
        return remote(
            send2.at[i, sides, rows], recv2.at[i, k - 1, sides],
            y2s.at[i, u, k - 1], y2r.at[i, u, k - 1], at_y(y + k, c),
        )

    def do_pair_sum(i, u, n):
        sib1(i, u, n).wait_recv()

        @pl.loop(0, n * QTR // SUB)
        def _(b):
            v = u + b // (QTR // SUB)
            rows = pl.ds(pl.multiple_of((b % (QTR // SUB)) * SUB, SUB), SUB)
            total = pre[i, v, rows, :] + recv1[i, v, rows, :].astype(F32)
            pre[i, v, rows, :] = total
            send2[i, v, rows, :] = total.astype(BF)

        for k in (2, 1, 3):
            ycopy(i, u, n, k).start()

    myrow = pl.ds(pl.multiple_of(y * SUB, SUB), SUB)

    def agcopy(i, u, n, k):
        ref = act.at[i, pl.ds(u, n), myrow]
        return remote(ref, ref, ags.at[i, u, k - 1], agr.at[i, u, k - 1], at_y(y + k, c))

    def agarrive(i, u, n, k):
        rows = pl.ds(pl.multiple_of(((y + 4 - k) % 4) * SUB, SUB), SUB)
        ref = act.at[i, pl.ds(u, n), rows]
        return remote(ref, ref, ags.at[i, u, k - 1], agr.at[i, u, k - 1], at_y(y + k, c))

    def do_act(i, u, n):
        for k in (1, 3, 2):
            ycopy(i, u, n, k).wait_recv()
        for v in range(u, u + n):

            def summed(lo, hi):
                total = pre[i, v, myrow, lo:hi]
                for k in range(3):
                    total = total + recv2[i, k, v, :, lo:hi].astype(F32)
                return total

            gate, up, back = summed(0, C), summed(C, C2), summed(C2, C3)
            p = jax.nn.sigmoid(gate)
            gp = gate * p
            act[i, v, myrow, 0:C] = (back * up * p * (1.0 + gate * (1.0 - p))).astype(BF)
            act[i, v, myrow, C:C2] = (back * gp).astype(BF)
            act[i, v, myrow, C2:C3] = (gp * up).astype(BF)
        for k in (2, 1, 3):
            agcopy(i, u, n, k).start()

    def sib2(i, u, n):
        sides = pl.ds(u, n)
        return remote(
            act.at[i, sides, pl.ds(0, QTR)], act.at[i, sides, pl.ds(QTR, QTR)],
            s2s.at[i, u], s2r.at[i, u], sibling,
        )

    def do_share(i, u, n):
        for k in (1, 3, 2):
            agarrive(i, u, n, k).wait_recv()
        sib2(i, u, n).start()

    def act_of(i, lo, hi):
        return act[i, :, :, lo:hi].reshape(T, hi - lo)

    def do_d_tokens(i):
        @pl.when(i < SPLIT)
        def _():
            for u in range(2):
                sib2(i, u, 1).wait_recv()

        @pl.when(i >= SPLIT)
        def _():
            sib2(i, 0, 2).wait_recv()

        for n in range(4):
            cols = slice(n * 256, (n + 1) * 256)
            acc[:, cols] += dot_t(act_of(i, 0, C2), wgu[i, cols, :])

    def do_terms(i):
        for n in range(3):
            cols = slice(n * 256, (n + 1) * 256)
            z = dot(tg[0], fgu[i, :, cols])
            term = jnp.sum(act_of(i, n * 256, (n + 1) * 256).astype(F32) * z, axis=0, keepdims=True)
            gt[i, :, cols] = term
        for n in range(4):
            cols = slice(n * 256, (n + 1) * 256)
            z = dot(act_of(i, C2, C3), fd[i, :, cols])
            dterm[:, cols] += jnp.sum(tg[1, :, cols].astype(F32) * z, axis=0, keepdims=True)

    def ecopy(part, k):
        return remote(
            esend.at[rows_of(1 - part, x + k)], erecv.at[part, k - 1],
            es.at[part, k - 1], er.at[part, k - 1], at_x(x + k, zh),
        )

    ezcopy = remote(ezsend, ezrecv, ezs, ezr, at_x(x, 1 - zh))

    def start_d_tokens(part):
        for k in (2, 1, 3):
            rows = rows_of(1 - part, x + k)
            esend[rows, :] = acc[rows, :].astype(BF)
            ecopy(part, k).start()

    quant_gate_up(0, 0, KB)
    start_gather()
    quant_down(0)

    @pl.loop(1, N)
    def _(i):
        quant_gate_up(i, 0, KB // 2)

        @pl.when(i == 2)
        def _():
            do_pair_sum(0, 0, 1)
            do_pair_sum(1, 0, 1)

        @pl.when(i == 3)
        def _():
            do_act(1, 0, 1)
            do_pair_sum(2, 0, 1)
            wait_gather(1)
            do_forward(0, 1, 1)
            do_forward(1, 1, 1)

        @pl.when(i == 4)
        def _():
            do_pair_sum(3, 0, 2)
            do_act(0, 1, 1)
            do_share(0, 0, 1)

        quant_gate_up(i, KB // 2, KB)

        @pl.when(i == 3)
        def _():
            do_pair_sum(0, 1, 1)
            do_pair_sum(1, 1, 1)
            do_forward(2, 1, 1)

        @pl.when(i == 4)
        def _():
            do_act(1, 1, 1)
            do_share(1, 0, 1)

        quant_down(i)

        @pl.when(i == 1)
        def _():
            wait_gather(0)
            do_forward(0, 0, 1)
            do_forward(1, 0, 1)
            pass_gather()

        @pl.when(i == 2)
        def _():
            do_forward(2, 0, 1)
            do_act(0, 0, 1)

        @pl.when(i == 3)
        def _():
            do_pair_sum(2, 1, 1)
            do_act(2, 0, 1)

        @pl.when(i >= 3)
        def _():
            do_forward(i, 0, 2)

        @pl.when(i == 4)
        def _():
            do_act(2, 1, 1)
            do_share(2, 0, 1)
            do_share(0, 1, 1)
            do_pair_sum(4, 0, 2)

    @pl.loop(0, N)
    def _(i):
        @pl.when(i == 0)
        def _():
            do_share(1, 1, 1)

        @pl.when(i == 1)
        def _():
            do_act(3, 0, 2)
            do_share(2, 1, 1)

        @pl.when(i == 3)
        def _():
            do_act(4, 0, 2)
            do_share(3, 0, 2)

        @pl.when(i == 4)
        def _():
            do_share(4, 0, 2)

        do_d_tokens(i)

        @pl.when(i == N - 1)
        def _():
            start_d_tokens(0)

        do_terms(i)

    gslot[din] = gt[...]
    dslot[x] = dterm[...]

    def gcopy(k):
        return remote(gt, gslot.at[din], gs_s.at[k - 1], gs_r.at[din], (dp, (din + k) % 8, dout))

    def garrive(k):
        src = (din + k) % 8
        return remote(gt, gslot.at[src], gs_s.at[k - 1], gs_r.at[src], (dp, src, dout))

    def dcopy(k):
        return remote(dterm, dslot.at[x], ds_s.at[k - 1], ds_r.at[x], at_x(x + k, zh))

    def darrive(k):
        src = (x + k) % 4
        return remote(dterm, dslot.at[src], ds_s.at[k - 1], ds_r.at[src], at_x(src, zh))

    for k in range(1, 4):
        dcopy(k).start()
    for k in range(1, 8):
        gcopy(k).start()
    start_d_tokens(1)
    for k in range(1, 4):
        ecopy(0, k).wait_recv()
    total = acc[theirs, :]
    for k in range(3):
        total = total + erecv[0, k].astype(F32)
    ezsend[...] = total.astype(BF)
    ezcopy.start()
    for k in range(1, 4):
        darrive(k).wait_recv()
    part = dslot[0]
    for k in range(1, 4):
        part = part + dslot[k]
    zi = zh * 4 + dp
    dz[zi] = part

    def at_z(k):
        return (k % 4, din, (k // 4) * 4 + x)

    def zzcopy(k):
        return remote(dz.at[zi], dz.at[zi], dz_s.at[k - 1], dz_r.at[zi], at_z((zi + k) % 8))

    def zzarrive(k):
        src = (zi + k) % 8
        return remote(dz.at[src], dz.at[src], dz_s.at[k - 1], dz_r.at[src], at_z(src))

    for k in range(1, 8):
        zzcopy(k).start()
    for k in range(1, 8):
        garrive(k).wait_recv()
    part = gslot[0]
    for k in range(1, 8):
        part = part + gslot[k]
    gdp[dp] = part

    def gpcopy(k):
        return remote(gdp.at[dp], gdp.at[dp], gp_s.at[k - 1], gp_r.at[dp], ((dp + k) % 4, din, dout))

    def gparrive(k):
        src = (dp + k) % 4
        return remote(gdp.at[src], gdp.at[src], gp_s.at[k - 1], gp_r.at[src], (src, din, dout))

    for k in range(1, 4):
        gpcopy(k).start()
    for k in range(1, 4):
        ecopy(1, k).wait_recv()
    total = acc[mine, :]
    for k in range(3):
        total = total + erecv[1, k].astype(F32)
    ezcopy.wait_recv()
    dt_out[...] = (total + ezrecv[...].astype(F32)).astype(BF)
    for k in range(1, 4):
        gparrive(k).wait_recv()
    part = gdp[0]
    for k in range(1, 4):
        part = part + gdp[k]
    gu_out[...] = part * SCALE_IN
    for k in range(1, 8):
        zzarrive(k).wait_recv()
    part = dz[0]
    for k in range(1, 8):
        part = part + dz[k]
    dg_out[...] = part * SCALE_HID

    zcopy.wait_send()
    ezcopy.wait_send()
    for k in range(1, 4):
        for which in range(2):
            xcopy(which, k).wait_send()
            ecopy(which, k).wait_send()
        dcopy(k).wait_send()
        gpcopy(k).wait_send()
    for k in range(1, 8):
        gcopy(k).wait_send()
        zzcopy(k).wait_send()

    for i in range(N):
        for u, n in ((0, 1), (1, 1)) if i < SPLIT else ((0, 2),):
            sib1(i, u, n).wait_send()
            sib2(i, u, n).wait_send()
            for k in range(1, 4):
                ycopy(i, u, n, k).wait_send()
                agcopy(i, u, n, k).wait_send()


def place(dt, gu, dg, dt_out, gg_out, ug_out, dg_out):
    dt_out[...] = dt[...]
    for i in range(N):
        gg_out[i * C : (i + 1) * C] = gu[i, :, 0:C].reshape(C)
        ug_out[i * C : (i + 1) * C] = gu[i, :, C:C2].reshape(C)
    dg_out[...] = dg[...].reshape(KB)


def shards(tokens, out_grad, gate_weight, up_weight, down_weight, gate_step, up_step, down_step, outlier_in, outlier_hidden):
    hbm = pl.BlockSpec(memory_space=pl.ANY)
    vmem = pl.BlockSpec(memory_space=pltpu.VMEM)
    smem = pl.BlockSpec(memory_space=pltpu.SMEM)
    V, S = pltpu.VMEM, pltpu.SemaphoreType.DMA
    results = pl.pallas_call(
        kernel,
        out_shape=(
            jax.ShapeDtypeStruct((BLK, KB), BF),
            jax.ShapeDtypeStruct((N, 1, C2), F32),
            jax.ShapeDtypeStruct((1, KB), F32),
        ),
        in_specs=[hbm, hbm, hbm, hbm, hbm, vmem, vmem, vmem, smem, smem],
        out_specs=(vmem, vmem, vmem),
        scratch_shapes=[
            V((2, T, KB), BF),
            V((N, KB, C2), BF),
            V((N, KB, C2), BF),
            V((N, C, KB), BF),
            V((N, C, KB), BF),
            V((KB, 128), F32),
            V((HB, 128), F32),
            V((N, 1, C2), F32),
            V((N, 1, C2), F32),
            V((1, KB), F32),
            V((1, KB), F32),
            V((N, 2, QTR, C3), F32),
            V((N, 2, QTR, C3), BF),
            V((N, 2, QTR, C3), BF),
            V((N, 2, QTR, C3), BF),
            V((N, 3, 2, SUB, C3), BF),
            V((N, 2, HALF, C3), BF),
            V((T, KB), F32),
            V((T, KB), BF),
            V((2, 3, BLK, KB), BF),
            V((BLK, KB), BF),
            V((BLK, KB), BF),
            V((N, 1, C2), F32),
            V((8, N, 1, C2), F32),
            V((4, N, 1, C2), F32),
            V((1, KB), F32),
            V((4, 1, KB), F32),
            V((8, 1, KB), F32),
            S((2,)),
            S((N, 2)),
            S((N,)),
            S, S,
            S((2, 3)), S((2, 3)),
            S((N, 2)), S((N, 2)),
            S((N, 2, 3)), S((N, 2, 3)),
            S((N, 2, 3)), S((N, 2, 3)),
            S((N, 2)), S((N, 2)),
            S((2, 3)), S((2, 3)),
            S, S,
            S((7,)), S((8,)),
            S((3,)), S((4,)),
            S((3,)), S((4,)),
            S((7,)), S((8,)),
        ],
        compiler_params=pltpu.CompilerParams(
            collective_id=0, has_side_effects=True, vmem_limit_bytes=56 * 2**20
        ),
        name="swiglu_back",
    )(
        tokens, out_grad, gate_weight, up_weight, down_weight,
        gate_step, up_step, down_step,
        outlier_in, outlier_hidden,
    )
    return pl.pallas_call(
        place,
        out_shape=(
            jax.ShapeDtypeStruct((BLK, KB), BF),
            jax.ShapeDtypeStruct((HB,), F32),
            jax.ShapeDtypeStruct((HB,), F32),
            jax.ShapeDtypeStruct((KB,), F32),
        ),
        in_specs=[vmem] * 3,
        out_specs=(vmem,) * 4,
        name="place",
    )(*results)


def solution(mesh):
    return jax.shard_map(
        shards,
        mesh=mesh,
        in_specs=(
            P(("dp", "dout"), "din"),
            P(("dp", "dout"), "din"),
            P("din", "dout"),
            P("din", "dout"),
            P("dout", "din"),
            P("dout"),
            P("dout"),
            P("din"),
            P("din"),
            P("dout"),
        ),
        out_specs=(P(("dp", "dout"), "din"), P("dout"), P("dout"), P("din")),
        check_vma=False,
    )
```

```python
import math

import jax
import jax.numpy as jnp
from jax import lax
from jax.experimental import pallas as pl
from jax.experimental.pallas import tpu as pltpu
from jax.sharding import PartitionSpec as P

D = 8192
FF = 15360
TOK_DEV = 256
SCALE_IN = 1.0 / math.sqrt(D * TOK_DEV)
SCALE_HID = 1.0 / math.sqrt(FF * TOK_DEV)

KB = 1024
HB = 1920
N = 5
C = HB // N
C2, C3 = 2 * C, 3 * C
T = 256
HALF = T // 2
BLK = 32
QTR = 64
SUB = 16
SPLIT = 3

MESH = pl.DeviceIdType.MESH
BF, F32 = jnp.bfloat16, jnp.float32

K = 0.9 / math.pi
SIN = tuple(math.sqrt(K) * v for v in (3.14158202, -5.16714276, 2.5418987, -0.55463534))


def quant(w, step, inv7, keep):
    w = w.astype(F32)
    x = w * inv7
    t = jnp.tanh(x)
    c = 7.0 * t
    r = c - jnp.round(c)
    u = r * r
    p = jnp.float32(SIN[3])
    for k in (2, 1, 0):
        p = p * u + jnp.float32(SIN[k])
    sn = p * r
    s2 = sn * sn
    d = jnp.maximum(K - s2, 1e-12)
    cs = d * lax.rsqrt(d)
    shaped = c - sn * cs
    slope7 = (0.7 + (12.6 / K) * s2) * (1.0 - t * t)
    q = jnp.where(keep, w, step * shaped)
    f = jnp.where(keep, 0.0, shaped - x * slope7)
    return q.astype(BF), f.astype(BF)


def remote(src, dst, ssem, rsem, dev):
    return pltpu.make_async_remote_copy(
        src_ref=src, dst_ref=dst, send_sem=ssem, recv_sem=rsem, device_id=dev, device_id_type=MESH
    )


def dot(a, b):
    return jnp.dot(a, b, preferred_element_type=F32)


def dot_t(a, b):
    return lax.dot_general(a, b, (((1,), (1,)), ((), ())), preferred_element_type=F32)


def kernel(
    tok_hbm, og_hbm, gw, uw, dw, gs, us, ds, oi, oh,
    dt_out, gu_out, dg_out,
    tg, wgu, fgu, wd, fd, kin, khid, sgu, igu, sdn, idn,
    pre, send1, recv1, send2, recv2, act,
    acc, esend, erecv, ezsend, ezrecv, gt, gslot, gdp, dterm, dslot, dz,
    lsem, gusem, dsem, zs, zr, xs, xr, s1s, s1r, y2s, y2r, ags, agr, s2s, s2r,
    es, er, ezs, ezr, gs_s, gs_r, gp_s, gp_r, ds_s, ds_r, dz_s, dz_r,
):
    dp = lax.axis_index("dp")
    din = lax.axis_index("din")
    dout = lax.axis_index("dout")
    y, c = din // 2, din % 2
    zh, x = dout // 4, dout % 4

    def at_y(k, core):
        return (dp, (k % 4) * 2 + core, dout)

    def at_x(k, hi):
        return (dp, din, hi * 4 + k % 4)

    sibling = (dp, y * 2 + (1 - c), dout)

    def rows_of(side, k):
        return pl.ds(pl.multiple_of(side * HALF + ((k % 4) * BLK + c * QTR) % HALF, BLK), BLK)

    barrier = pltpu.get_barrier_semaphore()

    def greet(dev):
        pl.semaphore_signal(barrier, inc=1, device_id=dev, device_id_type=MESH)

    for k in range(1, 8):
        greet((dp, (din + k) % 8, dout))
        greet((dp, din, (dout + k) % 8))
    for k in range(1, 4):
        greet(((dp + k) % 4, din, dout))
        greet(((dp + k) % 4, din, (dout + 4) % 8))

    mine = rows_of(0, x)
    own = [
        pltpu.make_async_copy(tok_hbm, tg.at[0, mine], lsem.at[0]),
        pltpu.make_async_copy(og_hbm, tg.at[1, mine], lsem.at[1]),
    ]
    for cp in own:
        cp.start()

    def weight_copies(i):
        cols = pl.ds(pl.multiple_of(i * C, 128), C)
        return [
            pltpu.make_async_copy(gw.at[:, cols], wgu.at[i, :, pl.ds(0, C)], gusem.at[i, 0]),
            pltpu.make_async_copy(uw.at[:, cols], wgu.at[i, :, pl.ds(C, C)], gusem.at[i, 1]),
        ]

    def down_copy(i):
        rows = pl.ds(pl.multiple_of(i * C, 128), C)
        return pltpu.make_async_copy(dw.at[rows], wd.at[i], dsem.at[i])

    @pl.loop(0, N)
    def _(i):
        for cp in weight_copies(i):
            cp.start()
        down_copy(i).start()

    def fill_mask(ref, values, start, rows, block):
        lane = lax.broadcasted_iota(jnp.int32, (block, 128), 1)
        row = lax.broadcasted_iota(jnp.int32, (block, 128), 0)
        listed = jnp.full((1, 128), -1, jnp.int32)
        for k in range(16):
            listed = jnp.where(lane[:1] == k, values[k] - start, listed)
        ones = jnp.ones((128, 128), BF)

        @pl.loop(0, rows // block)
        def _(b):
            hit = jnp.where(row + b * block == listed, 1.0, 0.0).astype(BF)
            ref[pl.ds(pl.multiple_of(b * block, block), block), :] = dot(hit, ones)

    fill_mask(kin, oi, din * KB, KB, 256)
    fill_mask(khid, oh, dout * HB, HB, 384)
    acc[...] = jnp.zeros_like(acc)
    for i in range(N):
        sgu[i, :, 0:C] = gs[i * C : (i + 1) * C].reshape(1, C)
        sgu[i, :, C:C2] = us[i * C : (i + 1) * C].reshape(1, C)
    sdn[...] = ds[...].reshape(1, KB)
    igu[...] = 1.0 / (7.0 * sgu[...])
    idn[...] = 1.0 / (7.0 * sdn[...])
    dterm[...] = jnp.zeros_like(dterm)

    theirs = rows_of(1, x)
    zcopy = remote(tg.at[:, mine], tg.at[:, theirs], zs, zr, at_x(x, 1 - zh))

    def xcopy(which, k):
        rows = mine if which == 0 else theirs
        return remote(tg.at[:, rows], tg.at[:, rows], xs.at[which, k - 1], xr.at[which, k - 1], at_x(x + k, zh))

    def xarrive(which, k):
        rows = rows_of(which, x + 4 - k)
        return remote(tg.at[:, rows], tg.at[:, rows], xs.at[which, k - 1], xr.at[which, k - 1], at_x(x + k, zh))

    def start_gather():
        pl.semaphore_wait(barrier, 20)
        for cp in own:
            cp.wait()
        zcopy.start()
        for k in (1, 3, 2):
            xcopy(0, k).start()

    def pass_gather():
        zcopy.wait_recv()
        for k in (1, 3, 2):
            xcopy(1, k).start()

    def wait_gather(which):
        for k in (1, 3, 2):
            xarrive(which, k).wait_recv()

    BOTH, FIRST, SECOND = 0, 1, 2

    def quant_rows(w_ref, f_ref, i, keep_ref, keep_at, lo, hi, width, step_of, inv_of, part):
        def body(b, carry):
            at = pl.ds(pl.multiple_of(b * 128, 128), 128)
            keep = keep_ref[pl.ds(pl.multiple_of(keep_at + b * 128, 128), 128), :] > 0
            for strip in range(width // 128):
                lanes = pl.ds(strip * 128, 128)
                w = (f_ref if part == SECOND else w_ref)[i, at, lanes]
                q, f = quant(w, step_of(lanes), inv_of(lanes), keep)
                if part != SECOND:
                    w_ref[i, at, lanes] = q
                f_ref[i, at, lanes] = w if part == FIRST else f
            return carry

        lax.fori_loop(lo // 128, hi // 128, body, 0)

    def quant_gate_up(i, lo, hi, part=BOTH):
        if lo == 0 and part != SECOND:
            for cp in weight_copies(i):
                cp.wait()
        quant_rows(wgu, fgu, i, kin, 0, lo, hi, C2, lambda l: sgu[i, :, l], lambda l: igu[i, :, l], part)

    def quant_down(i, part=BOTH):
        if part != SECOND:
            down_copy(i).wait()
        quant_rows(wd, fd, i, khid, i * C, 0, C, KB, lambda l: sdn[:, l], lambda l: idn[:, l], part)

    def sib1(i, u, n):
        sides = pl.ds(u, n)
        return remote(send1.at[i, sides], recv1.at[i, sides], s1s.at[i, u], s1r.at[i, u], sibling)

    def do_forward(i, u, n):
        def put(z, cols):
            for v in range(n):
                pre[i, u + v, :, cols] = z[v * HALF : v * HALF + QTR]
                send1[i, u + v, :, cols] = z[v * HALF + QTR : (v + 1) * HALF].astype(BF)

        tokens = slice(u * HALF, (u + n) * HALF)
        for k in range(3):
            cols = slice(k * 256, (k + 1) * 256)
            put(dot(tg[0, tokens], wgu[i, :, cols]), cols)
        put(dot_t(tg[1, tokens], wd[i]), slice(C2, C3))
        sib1(i, u, n).start()

    def ycopy(i, u, n, k):
        sides = pl.ds(u, n)
        rows = pl.ds(pl.multiple_of(((y + k) % 4) * SUB, SUB), SUB)
        return remote(
            send2.at[i, sides, rows], recv2.at[i, k - 1, sides],
            y2s.at[i, u, k - 1], y2r.at[i, u, k - 1], at_y(y + k, c),
        )

    def do_pair_sum(i, u, n):
        sib1(i, u, n).wait_recv()

        @pl.loop(0, n * QTR // SUB)
        def _(b):
            v = u + b // (QTR // SUB)
            rows = pl.ds(pl.multiple_of((b % (QTR // SUB)) * SUB, SUB), SUB)
            total = pre[i, v, rows, :] + recv1[i, v, rows, :].astype(F32)
            pre[i, v, rows, :] = total
            send2[i, v, rows, :] = total.astype(BF)

        for k in (2, 1, 3):
            ycopy(i, u, n, k).start()

    myrow = pl.ds(pl.multiple_of(y * SUB, SUB), SUB)

    def agcopy(i, u, n, k):
        ref = act.at[i, pl.ds(u, n), myrow]
        return remote(ref, ref, ags.at[i, u, k - 1], agr.at[i, u, k - 1], at_y(y + k, c))

    def agarrive(i, u, n, k):
        rows = pl.ds(pl.multiple_of(((y + 4 - k) % 4) * SUB, SUB), SUB)
        ref = act.at[i, pl.ds(u, n), rows]
        return remote(ref, ref, ags.at[i, u, k - 1], agr.at[i, u, k - 1], at_y(y + k, c))

    def do_act(i, u, n):
        for k in (1, 3, 2):
            ycopy(i, u, n, k).wait_recv()
        for v in range(u, u + n):

            def summed(lo, hi):
                total = pre[i, v, myrow, lo:hi]
                for k in range(3):
                    total = total + recv2[i, k, v, :, lo:hi].astype(F32)
                return total

            gate, up, back = summed(0, C), summed(C, C2), summed(C2, C3)
            p = jax.nn.sigmoid(gate)
            gp = gate * p
            act[i, v, myrow, 0:C] = (back * up * p * (1.0 + gate * (1.0 - p))).astype(BF)
            act[i, v, myrow, C:C2] = (back * gp).astype(BF)
            act[i, v, myrow, C2:C3] = (gp * up).astype(BF)
        for k in (2, 1, 3):
            agcopy(i, u, n, k).start()

    def sib2(i, u, n):
        sides = pl.ds(u, n)
        return remote(
            act.at[i, sides, pl.ds(0, QTR)], act.at[i, sides, pl.ds(QTR, QTR)],
            s2s.at[i, u], s2r.at[i, u], sibling,
        )

    def do_share(i, u, n):
        for k in (1, 3, 2):
            agarrive(i, u, n, k).wait_recv()
        sib2(i, u, n).start()

    def act_of(i, lo, hi):
        return act[i, :, :, lo:hi].reshape(T, hi - lo)

    def wait_share(i):
        @pl.when(i < SPLIT)
        def _():
            for u in range(2):
                sib2(i, u, 1).wait_recv()

        @pl.when(i >= SPLIT)
        def _():
            sib2(i, 0, 2).wait_recv()

    def do_d_tokens(i):
        for n in range(4):
            cols = slice(n * 256, (n + 1) * 256)
            acc[:, cols] += dot_t(act_of(i, 0, C2), wgu[i, cols, :])

    def do_terms(i):
        for n in range(3):
            cols = slice(n * 256, (n + 1) * 256)
            z = dot(tg[0], fgu[i, :, cols])
            term = jnp.sum(act_of(i, n * 256, (n + 1) * 256).astype(F32) * z, axis=0, keepdims=True)
            gt[i, :, cols] = term
        for n in range(4):
            cols = slice(n * 256, (n + 1) * 256)
            z = dot(act_of(i, C2, C3), fd[i, :, cols])
            dterm[:, cols] += jnp.sum(tg[1, :, cols].astype(F32) * z, axis=0, keepdims=True)

    def ecopy(part, k):
        return remote(
            esend.at[rows_of(1 - part, x + k)], erecv.at[part, k - 1],
            es.at[part, k - 1], er.at[part, k - 1], at_x(x + k, zh),
        )

    ezcopy = remote(ezsend, ezrecv, ezs, ezr, at_x(x, 1 - zh))

    def start_d_tokens(part):
        for k in (2, 1, 3):
            rows = rows_of(1 - part, x + k)
            esend[rows, :] = acc[rows, :].astype(BF)
            ecopy(part, k).start()

    quant_gate_up(0, 0, KB)
    start_gather()
    quant_down(0)

    @pl.loop(1, N - 1)
    def _(i):
        quant_gate_up(i, 0, KB // 2)

        @pl.when(i == 2)
        def _():
            do_pair_sum(0, 0, 1)
            do_pair_sum(1, 0, 1)

        @pl.when(i == 3)
        def _():
            do_act(1, 0, 1)
            do_pair_sum(2, 0, 1)
            wait_gather(1)
            do_forward(0, 1, 1)
            do_forward(1, 1, 1)

        quant_gate_up(i, KB // 2, KB)

        @pl.when(i == 3)
        def _():
            do_pair_sum(0, 1, 1)
            do_pair_sum(1, 1, 1)
            do_forward(2, 1, 1)

        quant_down(i)

        @pl.when(i == 1)
        def _():
            wait_gather(0)
            do_forward(0, 0, 1)
            do_forward(1, 0, 1)
            pass_gather()

        @pl.when(i == 2)
        def _():
            do_forward(2, 0, 1)
            do_act(0, 0, 1)

        @pl.when(i == 3)
        def _():
            do_pair_sum(2, 1, 1)
            do_act(2, 0, 1)
            do_forward(3, 0, 2)

    last = N - 1
    quant_gate_up(last, 0, KB // 2, FIRST)
    do_pair_sum(3, 0, 2)
    do_act(0, 1, 1)
    do_share(0, 0, 1)
    quant_gate_up(last, KB // 2, KB, FIRST)
    do_act(1, 1, 1)
    do_share(1, 0, 1)
    quant_down(last, FIRST)
    do_forward(last, 0, 2)
    do_act(2, 1, 1)
    do_share(2, 0, 1)
    quant_gate_up(last, 0, KB // 2, SECOND)
    do_pair_sum(last, 0, 2)
    do_act(3, 0, 2)
    quant_gate_up(last, KB // 2, KB, SECOND)
    do_share(0, 1, 1)
    do_share(1, 1, 1)

    @pl.loop(0, last)
    def _(i):
        @pl.when(i == 1)
        def _():
            do_share(2, 1, 1)

        @pl.when(i == 2)
        def _():
            do_act(last, 0, 2)

        @pl.when(i == 3)
        def _():
            quant_down(last, SECOND)
            do_share(3, 0, 2)
            do_share(last, 0, 2)

        wait_share(i)
        do_d_tokens(i)
        do_terms(i)

    wait_share(last)
    do_d_tokens(last)
    start_d_tokens(0)
    do_terms(last)

    gslot[din] = gt[...]
    dslot[x] = dterm[...]

    def gcopy(k):
        return remote(gt, gslot.at[din], gs_s.at[k - 1], gs_r.at[din], (dp, (din + k) % 8, dout))

    def garrive(k):
        src = (din + k) % 8
        return remote(gt, gslot.at[src], gs_s.at[k - 1], gs_r.at[src], (dp, src, dout))

    def dcopy(k):
        return remote(dterm, dslot.at[x], ds_s.at[k - 1], ds_r.at[x], at_x(x + k, zh))

    def darrive(k):
        src = (x + k) % 4
        return remote(dterm, dslot.at[src], ds_s.at[k - 1], ds_r.at[src], at_x(src, zh))

    for k in range(1, 4):
        dcopy(k).start()
    for k in range(1, 8):
        gcopy(k).start()
    start_d_tokens(1)
    for k in range(1, 8):
        garrive(k).wait_recv()
    part = gslot[0]
    for k in range(1, 8):
        part = part + gslot[k]
    gdp[dp] = part

    def gpcopy(k):
        return remote(gdp.at[dp], gdp.at[dp], gp_s.at[k - 1], gp_r.at[dp], ((dp + k) % 4, din, dout))

    def gparrive(k):
        src = (dp + k) % 4
        return remote(gdp.at[src], gdp.at[src], gp_s.at[k - 1], gp_r.at[src], (src, din, dout))

    for k in range(1, 4):
        gpcopy(k).start()
    for k in range(1, 4):
        darrive(k).wait_recv()
    part = dslot[0]
    for k in range(1, 4):
        part = part + dslot[k]
    zi = zh * 4 + dp
    dz[zi] = part

    def at_z(k):
        return (k % 4, din, (k // 4) * 4 + x)

    def zzcopy(k):
        return remote(dz.at[zi], dz.at[zi], dz_s.at[k - 1], dz_r.at[zi], at_z((zi + k) % 8))

    def zzarrive(k):
        src = (zi + k) % 8
        return remote(dz.at[src], dz.at[src], dz_s.at[k - 1], dz_r.at[src], at_z(src))

    for k in range(1, 8):
        zzcopy(k).start()
    for k in range(1, 4):
        ecopy(0, k).wait_recv()
    total = acc[theirs, :]
    for k in range(3):
        total = total + erecv[0, k].astype(F32)
    ezsend[...] = total.astype(BF)
    ezcopy.start()
    for k in range(1, 4):
        ecopy(1, k).wait_recv()
    total = acc[mine, :]
    for k in range(3):
        total = total + erecv[1, k].astype(F32)
    ezcopy.wait_recv()
    dt_out[...] = (total + ezrecv[...].astype(F32)).astype(BF)
    for k in range(1, 4):
        gparrive(k).wait_recv()
    part = gdp[0]
    for k in range(1, 4):
        part = part + gdp[k]
    gu_out[...] = part * SCALE_IN
    for k in range(1, 8):
        zzarrive(k).wait_recv()
    part = dz[0]
    for k in range(1, 8):
        part = part + dz[k]
    dg_out[...] = part * SCALE_HID

    zcopy.wait_send()
    ezcopy.wait_send()
    for k in range(1, 4):
        for which in range(2):
            xcopy(which, k).wait_send()
            ecopy(which, k).wait_send()
        dcopy(k).wait_send()
        gpcopy(k).wait_send()
    for k in range(1, 8):
        gcopy(k).wait_send()
        zzcopy(k).wait_send()

    for i in range(N):
        for u, n in ((0, 1), (1, 1)) if i < SPLIT else ((0, 2),):
            sib1(i, u, n).wait_send()
            sib2(i, u, n).wait_send()
            for k in range(1, 4):
                ycopy(i, u, n, k).wait_send()
                agcopy(i, u, n, k).wait_send()


def place(dt, gu, dg, dt_out, gg_out, ug_out, dg_out):
    dt_out[...] = dt[...]
    for i in range(N):
        gg_out[i * C : (i + 1) * C] = gu[i, :, 0:C].reshape(C)
        ug_out[i * C : (i + 1) * C] = gu[i, :, C:C2].reshape(C)
    dg_out[...] = dg[...].reshape(KB)


def shards(tokens, out_grad, gate_weight, up_weight, down_weight, gate_step, up_step, down_step, outlier_in, outlier_hidden):
    hbm = pl.BlockSpec(memory_space=pl.ANY)
    vmem = pl.BlockSpec(memory_space=pltpu.VMEM)
    smem = pl.BlockSpec(memory_space=pltpu.SMEM)
    V, S = pltpu.VMEM, pltpu.SemaphoreType.DMA
    results = pl.pallas_call(
        kernel,
        out_shape=(
            jax.ShapeDtypeStruct((BLK, KB), BF),
            jax.ShapeDtypeStruct((N, 1, C2), F32),
            jax.ShapeDtypeStruct((1, KB), F32),
        ),
        in_specs=[hbm, hbm, hbm, hbm, hbm, vmem, vmem, vmem, smem, smem],
        out_specs=(vmem, vmem, vmem),
        scratch_shapes=[
            V((2, T, KB), BF),
            V((N, KB, C2), BF),
            V((N, KB, C2), BF),
            V((N, C, KB), BF),
            V((N, C, KB), BF),
            V((KB, 128), F32),
            V((HB, 128), F32),
            V((N, 1, C2), F32),
            V((N, 1, C2), F32),
            V((1, KB), F32),
            V((1, KB), F32),
            V((N, 2, QTR, C3), F32),
            V((N, 2, QTR, C3), BF),
            V((N, 2, QTR, C3), BF),
            V((N, 2, QTR, C3), BF),
            V((N, 3, 2, SUB, C3), BF),
            V((N, 2, HALF, C3), BF),
            V((T, KB), F32),
            V((T, KB), BF),
            V((2, 3, BLK, KB), BF),
            V((BLK, KB), BF),
            V((BLK, KB), BF),
            V((N, 1, C2), F32),
            V((8, N, 1, C2), F32),
            V((4, N, 1, C2), F32),
            V((1, KB), F32),
            V((4, 1, KB), F32),
            V((8, 1, KB), F32),
            S((2,)),
            S((N, 2)),
            S((N,)),
            S, S,
            S((2, 3)), S((2, 3)),
            S((N, 2)), S((N, 2)),
            S((N, 2, 3)), S((N, 2, 3)),
            S((N, 2, 3)), S((N, 2, 3)),
            S((N, 2)), S((N, 2)),
            S((2, 3)), S((2, 3)),
            S, S,
            S((7,)), S((8,)),
            S((3,)), S((4,)),
            S((3,)), S((4,)),
            S((7,)), S((8,)),
        ],
        compiler_params=pltpu.CompilerParams(
            collective_id=0, has_side_effects=True, vmem_limit_bytes=56 * 2**20
        ),
        name="swiglu_back",
    )(
        tokens, out_grad, gate_weight, up_weight, down_weight,
        gate_step, up_step, down_step,
        outlier_in, outlier_hidden,
    )
    return pl.pallas_call(
        place,
        out_shape=(
            jax.ShapeDtypeStruct((BLK, KB), BF),
            jax.ShapeDtypeStruct((HB,), F32),
            jax.ShapeDtypeStruct((HB,), F32),
            jax.ShapeDtypeStruct((KB,), F32),
        ),
        in_specs=[vmem] * 3,
        out_specs=(vmem,) * 4,
        name="place",
    )(*results)


def solution(mesh):
    return jax.shard_map(
        shards,
        mesh=mesh,
        in_specs=(
            P(("dp", "dout"), "din"),
            P(("dp", "dout"), "din"),
            P("din", "dout"),
            P("din", "dout"),
            P("dout", "din"),
            P("dout"),
            P("dout"),
            P("din"),
            P("din"),
            P("dout"),
        ),
        out_specs=(P(("dp", "dout"), "din"), P("dout"), P("dout"), P("din")),
        check_vma=False,
    )
```

```python
import math

import jax
import jax.numpy as jnp
from jax import lax
from jax.experimental import pallas as pl
from jax.experimental.pallas import tpu as pltpu
from jax.sharding import PartitionSpec as P

D = 8192
FF = 15360
TOK_DEV = 256
SCALE_IN = 1.0 / math.sqrt(D * TOK_DEV)
SCALE_HID = 1.0 / math.sqrt(FF * TOK_DEV)

KB = 1024
HB = 1920
N = 5
C = HB // N
C2, C3 = 2 * C, 3 * C
T = 256
HALF = T // 2
BLK = 32
QTR = 64
SUB = 16
SPLIT = 3

MESH = pl.DeviceIdType.MESH
BF, F32 = jnp.bfloat16, jnp.float32

K = 0.9 / math.pi
SIN = tuple(math.sqrt(K) * v for v in (3.14158202, -5.16714276, 2.5418987, -0.55463534))


def quant(w, step, inv7, keep):
    w = w.astype(F32)
    x = w * inv7
    t = jnp.tanh(x)
    c = 7.0 * t
    r = c - jnp.round(c)
    u = r * r
    p = jnp.float32(SIN[3])
    for k in (2, 1, 0):
        p = p * u + jnp.float32(SIN[k])
    sn = p * r
    s2 = sn * sn
    d = jnp.maximum(K - s2, 1e-12)
    cs = d * lax.rsqrt(d)
    shaped = c - sn * cs
    slope7 = (0.7 + (12.6 / K) * s2) * (1.0 - t * t)
    q = jnp.where(keep, w, step * shaped)
    f = jnp.where(keep, 0.0, shaped - x * slope7)
    return q.astype(BF), f.astype(BF)


def remote(src, dst, ssem, rsem, dev):
    return pltpu.make_async_remote_copy(
        src_ref=src, dst_ref=dst, send_sem=ssem, recv_sem=rsem, device_id=dev, device_id_type=MESH
    )


def dot(a, b):
    return jnp.dot(a, b, preferred_element_type=F32)


def dot_t(a, b):
    return lax.dot_general(a, b, (((1,), (1,)), ((), ())), preferred_element_type=F32)


def kernel(
    tok_hbm, og_hbm, gw, uw, dw, gs, us, ds, oi, oh,
    dt_out, gu_out, dg_out,
    tg, wgu, fgu, wd, fd, kin, khid, sgu, igu, sdn, idn,
    pre, send1, recv1, send2, recv2, act,
    acc, esend, erecv, ezsend, ezrecv, gt, gslot, gdp, dterm, dslot, dz,
    lsem, gusem, dsem, zs, zr, xs, xr, s1s, s1r, y2s, y2r, ags, agr, s2s, s2r,
    es, er, ezs, ezr, gs_s, gs_r, gp_s, gp_r, ds_s, ds_r, dz_s, dz_r,
):
    dp = lax.axis_index("dp")
    din = lax.axis_index("din")
    dout = lax.axis_index("dout")
    y, c = din // 2, din % 2
    zh, x = dout // 4, dout % 4

    def at_y(k, core):
        return (dp, (k % 4) * 2 + core, dout)

    def at_x(k, hi):
        return (dp, din, hi * 4 + k % 4)

    sibling = (dp, y * 2 + (1 - c), dout)

    def rows_of(side, k):
        return pl.ds(pl.multiple_of(side * HALF + ((k % 4) * BLK + c * QTR) % HALF, BLK), BLK)

    barrier = pltpu.get_barrier_semaphore()

    def greet(dev):
        pl.semaphore_signal(barrier, inc=1, device_id=dev, device_id_type=MESH)

    for k in range(1, 8):
        greet((dp, (din + k) % 8, dout))
        greet((dp, din, (dout + k) % 8))
    for k in range(1, 4):
        greet(((dp + k) % 4, din, dout))
        greet(((dp + k) % 4, din, (dout + 4) % 8))

    mine = rows_of(0, x)
    own = [
        pltpu.make_async_copy(tok_hbm, tg.at[0, mine], lsem.at[0]),
        pltpu.make_async_copy(og_hbm, tg.at[1, mine], lsem.at[1]),
    ]
    for cp in own:
        cp.start()

    def weight_copies(i):
        cols = pl.ds(pl.multiple_of(i * C, 128), C)
        return [
            pltpu.make_async_copy(gw.at[:, cols], wgu.at[i, :, pl.ds(0, C)], gusem.at[i, 0]),
            pltpu.make_async_copy(uw.at[:, cols], wgu.at[i, :, pl.ds(C, C)], gusem.at[i, 1]),
        ]

    def down_copy(i):
        rows = pl.ds(pl.multiple_of(i * C, 128), C)
        return pltpu.make_async_copy(dw.at[rows], wd.at[i], dsem.at[i])

    @pl.loop(0, N)
    def _(i):
        for cp in weight_copies(i):
            cp.start()
        down_copy(i).start()

    def fill_mask(ref, values, start, rows, block):
        lane = lax.broadcasted_iota(jnp.int32, (block, 128), 1)
        row = lax.broadcasted_iota(jnp.int32, (block, 128), 0)
        listed = jnp.full((1, 128), -1, jnp.int32)
        for k in range(16):
            listed = jnp.where(lane[:1] == k, values[k] - start, listed)
        ones = jnp.ones((128, 128), BF)

        @pl.loop(0, rows // block)
        def _(b):
            hit = jnp.where(row + b * block == listed, 1.0, 0.0).astype(BF)
            ref[pl.ds(pl.multiple_of(b * block, block), block), :] = dot(hit, ones)

    fill_mask(kin, oi, din * KB, KB, 256)
    fill_mask(khid, oh, dout * HB, HB, 384)
    acc[...] = jnp.zeros_like(acc)
    for i in range(N):
        sgu[i, :, 0:C] = gs[i * C : (i + 1) * C].reshape(1, C)
        sgu[i, :, C:C2] = us[i * C : (i + 1) * C].reshape(1, C)
    sdn[...] = ds[...].reshape(1, KB)
    igu[...] = 1.0 / (7.0 * sgu[...])
    idn[...] = 1.0 / (7.0 * sdn[...])
    dterm[...] = jnp.zeros_like(dterm)

    theirs = rows_of(1, x)
    zcopy = remote(tg.at[:, mine], tg.at[:, theirs], zs, zr, at_x(x, 1 - zh))

    def xcopy(which, k):
        rows = mine if which == 0 else theirs
        return remote(tg.at[:, rows], tg.at[:, rows], xs.at[which, k - 1], xr.at[which, k - 1], at_x(x + k, zh))

    def xarrive(which, k):
        rows = rows_of(which, x + 4 - k)
        return remote(tg.at[:, rows], tg.at[:, rows], xs.at[which, k - 1], xr.at[which, k - 1], at_x(x + k, zh))

    def start_gather():
        pl.semaphore_wait(barrier, 20)
        for cp in own:
            cp.wait()
        zcopy.start()
        for k in (1, 3, 2):
            xcopy(0, k).start()

    def pass_gather():
        zcopy.wait_recv()
        for k in (1, 3, 2):
            xcopy(1, k).start()

    def wait_gather(which):
        for k in (1, 3, 2):
            xarrive(which, k).wait_recv()

    BOTH, FIRST, SECOND = 0, 1, 2

    def quant_rows(w_ref, f_ref, i, keep_ref, keep_at, lo, hi, width, step_of, inv_of, part):
        def body(b, carry):
            at = pl.ds(pl.multiple_of(b * 128, 128), 128)
            keep = keep_ref[pl.ds(pl.multiple_of(keep_at + b * 128, 128), 128), :] > 0
            for strip in range(width // 128):
                lanes = pl.ds(strip * 128, 128)
                w = (f_ref if part == SECOND else w_ref)[i, at, lanes]
                q, f = quant(w, step_of(lanes), inv_of(lanes), keep)
                if part != SECOND:
                    w_ref[i, at, lanes] = q
                f_ref[i, at, lanes] = w if part == FIRST else f
            return carry

        lax.fori_loop(lo // 128, hi // 128, body, 0)

    def quant_gate_up(i, lo, hi, part=BOTH):
        if lo == 0 and part != SECOND:
            for cp in weight_copies(i):
                cp.wait()
        quant_rows(wgu, fgu, i, kin, 0, lo, hi, C2, lambda l: sgu[i, :, l], lambda l: igu[i, :, l], part)

    def quant_down(i, part=BOTH):
        if part != SECOND:
            down_copy(i).wait()
        quant_rows(wd, fd, i, khid, i * C, 0, C, KB, lambda l: sdn[:, l], lambda l: idn[:, l], part)

    def sib1(i, u, n):
        sides = pl.ds(u, n)
        return remote(send1.at[i, sides], recv1.at[i, sides], s1s.at[i, u], s1r.at[i, u], sibling)

    def do_forward(i, u, n):
        def put(z, cols):
            for v in range(n):
                pre[i, u + v, :, cols] = z[v * HALF : v * HALF + QTR]
                send1[i, u + v, :, cols] = z[v * HALF + QTR : (v + 1) * HALF].astype(BF)

        tokens = slice(u * HALF, (u + n) * HALF)
        for k in range(3):
            cols = slice(k * 256, (k + 1) * 256)
            put(dot(tg[0, tokens], wgu[i, :, cols]), cols)
        put(dot_t(tg[1, tokens], wd[i]), slice(C2, C3))
        sib1(i, u, n).start()

    def ycopy(i, u, n, k):
        sides = pl.ds(u, n)
        rows = pl.ds(pl.multiple_of(((y + k) % 4) * SUB, SUB), SUB)
        return remote(
            send2.at[i, sides, rows], recv2.at[i, k - 1, sides],
            y2s.at[i, u, k - 1], y2r.at[i, u, k - 1], at_y(y + k, c),
        )

    def do_pair_sum(i, u, n):
        sib1(i, u, n).wait_recv()

        @pl.loop(0, n * QTR // SUB)
        def _(b):
            v = u + b // (QTR // SUB)
            rows = pl.ds(pl.multiple_of((b % (QTR // SUB)) * SUB, SUB), SUB)
            total = pre[i, v, rows, :] + recv1[i, v, rows, :].astype(F32)
            pre[i, v, rows, :] = total
            send2[i, v, rows, :] = total.astype(BF)

        for k in (2, 1, 3):
            ycopy(i, u, n, k).start()

    myrow = pl.ds(pl.multiple_of(y * SUB, SUB), SUB)

    def agcopy(i, u, n, k):
        ref = act.at[i, pl.ds(u, n), myrow]
        return remote(ref, ref, ags.at[i, u, k - 1], agr.at[i, u, k - 1], at_y(y + k, c))

    def agarrive(i, u, n, k):
        rows = pl.ds(pl.multiple_of(((y + 4 - k) % 4) * SUB, SUB), SUB)
        ref = act.at[i, pl.ds(u, n), rows]
        return remote(ref, ref, ags.at[i, u, k - 1], agr.at[i, u, k - 1], at_y(y + k, c))

    def do_act(i, u, n):
        for k in (1, 3, 2):
            ycopy(i, u, n, k).wait_recv()
        for v in range(u, u + n):

            def summed(lo, hi):
                total = pre[i, v, myrow, lo:hi]
                for k in range(3):
                    total = total + recv2[i, k, v, :, lo:hi].astype(F32)
                return total

            gate, up, back = summed(0, C), summed(C, C2), summed(C2, C3)
            p = jax.nn.sigmoid(gate)
            gp = gate * p
            act[i, v, myrow, 0:C] = (back * up * p * (1.0 + gate * (1.0 - p))).astype(BF)
            act[i, v, myrow, C:C2] = (back * gp).astype(BF)
            act[i, v, myrow, C2:C3] = (gp * up).astype(BF)
        for k in (2, 1, 3):
            agcopy(i, u, n, k).start()

    def sib2(i, u, n):
        sides = pl.ds(u, n)
        return remote(
            act.at[i, sides, pl.ds(0, QTR)], act.at[i, sides, pl.ds(QTR, QTR)],
            s2s.at[i, u], s2r.at[i, u], sibling,
        )

    def do_share(i, u, n):
        for k in (1, 3, 2):
            agarrive(i, u, n, k).wait_recv()
        sib2(i, u, n).start()

    def act_of(i, lo, hi):
        return act[i, :, :, lo:hi].reshape(T, hi - lo)

    def wait_share(i):
        @pl.when(i < SPLIT)
        def _():
            for u in range(2):
                sib2(i, u, 1).wait_recv()

        @pl.when(i >= SPLIT)
        def _():
            sib2(i, 0, 2).wait_recv()

    def do_d_tokens(i):
        for n in range(4):
            cols = slice(n * 256, (n + 1) * 256)
            acc[:, cols] += dot_t(act_of(i, 0, C2), wgu[i, cols, :])

    def do_gate_terms(i):
        for n in range(3):
            cols = slice(n * 256, (n + 1) * 256)
            z = dot(tg[0], fgu[i, :, cols])
            term = jnp.sum(act_of(i, n * 256, (n + 1) * 256).astype(F32) * z, axis=0, keepdims=True)
            gt[i, :, cols] = term

    def do_down_terms(i):
        for n in range(4):
            cols = slice(n * 256, (n + 1) * 256)
            z = dot(act_of(i, C2, C3), fd[i, :, cols])
            dterm[:, cols] += jnp.sum(tg[1, :, cols].astype(F32) * z, axis=0, keepdims=True)

    def ecopy(part, k):
        return remote(
            esend.at[rows_of(1 - part, x + k)], erecv.at[part, k - 1],
            es.at[part, k - 1], er.at[part, k - 1], at_x(x + k, zh),
        )

    ezcopy = remote(ezsend, ezrecv, ezs, ezr, at_x(x, 1 - zh))

    def start_d_tokens(part):
        for k in (2, 1, 3):
            rows = rows_of(1 - part, x + k)
            esend[rows, :] = acc[rows, :].astype(BF)
            ecopy(part, k).start()

    quant_gate_up(0, 0, KB)
    start_gather()
    quant_down(0)

    @pl.loop(1, N - 1)
    def _(i):
        quant_gate_up(i, 0, KB // 2)

        @pl.when(i == 2)
        def _():
            do_pair_sum(0, 0, 1)
            do_pair_sum(1, 0, 1)

        @pl.when(i == 3)
        def _():
            do_act(1, 0, 1)
            do_pair_sum(2, 0, 1)
            wait_gather(1)
            do_forward(0, 1, 1)
            do_forward(1, 1, 1)

        quant_gate_up(i, KB // 2, KB)

        @pl.when(i == 3)
        def _():
            do_pair_sum(0, 1, 1)
            do_pair_sum(1, 1, 1)
            do_forward(2, 1, 1)

        quant_down(i)

        @pl.when(i == 1)
        def _():
            wait_gather(0)
            do_forward(0, 0, 1)
            do_forward(1, 0, 1)
            pass_gather()

        @pl.when(i == 2)
        def _():
            do_forward(2, 0, 1)
            do_act(0, 0, 1)

        @pl.when(i == 3)
        def _():
            do_pair_sum(2, 1, 1)
            do_act(2, 0, 1)
            do_forward(3, 0, 2)

    last = N - 1
    quant_gate_up(last, 0, KB // 2, FIRST)
    do_pair_sum(3, 0, 2)
    do_act(0, 1, 1)
    do_share(0, 0, 1)
    quant_gate_up(last, KB // 2, KB, FIRST)
    do_act(1, 1, 1)
    do_share(1, 0, 1)
    quant_down(last, FIRST)
    do_forward(last, 0, 2)
    do_act(2, 1, 1)
    do_share(2, 0, 1)
    quant_gate_up(last, 0, KB // 2, SECOND)
    do_pair_sum(last, 0, 2)
    do_act(3, 0, 2)
    quant_gate_up(last, KB // 2, KB, SECOND)
    do_share(0, 1, 1)
    do_share(1, 1, 1)

    @pl.loop(0, last)
    def _(i):
        @pl.when(i == 1)
        def _():
            do_share(2, 1, 1)

        @pl.when(i == 2)
        def _():
            do_act(last, 0, 2)

        @pl.when(i == 3)
        def _():
            quant_down(last, SECOND)
            do_share(3, 0, 2)
            do_share(last, 0, 2)

        wait_share(i)
        do_d_tokens(i)
        do_gate_terms(i)
        do_down_terms(i)

    wait_share(last)
    do_down_terms(last)

    dslot[x] = dterm[...]

    def gcopy(k):
        return remote(gt, gslot.at[din], gs_s.at[k - 1], gs_r.at[din], (dp, (din + k) % 8, dout))

    def garrive(k):
        src = (din + k) % 8
        return remote(gt, gslot.at[src], gs_s.at[k - 1], gs_r.at[src], (dp, src, dout))

    def dcopy(k):
        return remote(dterm, dslot.at[x], ds_s.at[k - 1], ds_r.at[x], at_x(x + k, zh))

    def darrive(k):
        src = (x + k) % 4
        return remote(dterm, dslot.at[src], ds_s.at[k - 1], ds_r.at[src], at_x(src, zh))

    for k in range(1, 4):
        dcopy(k).start()
    do_d_tokens(last)
    start_d_tokens(0)
    do_gate_terms(last)
    gslot[din] = gt[...]
    for k in range(1, 8):
        gcopy(k).start()
    start_d_tokens(1)
    for k in range(1, 4):
        darrive(k).wait_recv()
    part = dslot[0]
    for k in range(1, 4):
        part = part + dslot[k]
    zi = zh * 4 + dp
    dz[zi] = part

    def at_z(k):
        return (k % 4, din, (k // 4) * 4 + x)

    def zzcopy(k):
        return remote(dz.at[zi], dz.at[zi], dz_s.at[k - 1], dz_r.at[zi], at_z((zi + k) % 8))

    def zzarrive(k):
        src = (zi + k) % 8
        return remote(dz.at[src], dz.at[src], dz_s.at[k - 1], dz_r.at[src], at_z(src))

    for k in range(1, 8):
        zzcopy(k).start()
    for k in range(1, 8):
        garrive(k).wait_recv()
    part = gslot[0]
    for k in range(1, 8):
        part = part + gslot[k]
    gdp[dp] = part

    def gpcopy(k):
        return remote(gdp.at[dp], gdp.at[dp], gp_s.at[k - 1], gp_r.at[dp], ((dp + k) % 4, din, dout))

    def gparrive(k):
        src = (dp + k) % 4
        return remote(gdp.at[src], gdp.at[src], gp_s.at[k - 1], gp_r.at[src], (src, din, dout))

    for k in range(1, 4):
        gpcopy(k).start()
    for k in range(1, 4):
        ecopy(0, k).wait_recv()
    total = acc[theirs, :]
    for k in range(3):
        total = total + erecv[0, k].astype(F32)
    ezsend[...] = total.astype(BF)
    ezcopy.start()
    for k in range(1, 4):
        ecopy(1, k).wait_recv()
    total = acc[mine, :]
    for k in range(3):
        total = total + erecv[1, k].astype(F32)
    ezcopy.wait_recv()
    dt_out[...] = (total + ezrecv[...].astype(F32)).astype(BF)
    for k in range(1, 4):
        gparrive(k).wait_recv()
    part = gdp[0]
    for k in range(1, 4):
        part = part + gdp[k]
    gu_out[...] = part * SCALE_IN
    for k in range(1, 8):
        zzarrive(k).wait_recv()
    part = dz[0]
    for k in range(1, 8):
        part = part + dz[k]
    dg_out[...] = part * SCALE_HID

    zcopy.wait_send()
    ezcopy.wait_send()
    for k in range(1, 4):
        for which in range(2):
            xcopy(which, k).wait_send()
            ecopy(which, k).wait_send()
        dcopy(k).wait_send()
        gpcopy(k).wait_send()
    for k in range(1, 8):
        gcopy(k).wait_send()
        zzcopy(k).wait_send()

    for i in range(N):
        for u, n in ((0, 1), (1, 1)) if i < SPLIT else ((0, 2),):
            sib1(i, u, n).wait_send()
            sib2(i, u, n).wait_send()
            for k in range(1, 4):
                ycopy(i, u, n, k).wait_send()
                agcopy(i, u, n, k).wait_send()


def place(dt, gu, dg, dt_out, gg_out, ug_out, dg_out):
    dt_out[...] = dt[...]
    for i in range(N):
        gg_out[i * C : (i + 1) * C] = gu[i, :, 0:C].reshape(C)
        ug_out[i * C : (i + 1) * C] = gu[i, :, C:C2].reshape(C)
    dg_out[...] = dg[...].reshape(KB)


def shards(tokens, out_grad, gate_weight, up_weight, down_weight, gate_step, up_step, down_step, outlier_in, outlier_hidden):
    hbm = pl.BlockSpec(memory_space=pl.ANY)
    vmem = pl.BlockSpec(memory_space=pltpu.VMEM)
    smem = pl.BlockSpec(memory_space=pltpu.SMEM)
    V, S = pltpu.VMEM, pltpu.SemaphoreType.DMA
    results = pl.pallas_call(
        kernel,
        out_shape=(
            jax.ShapeDtypeStruct((BLK, KB), BF),
            jax.ShapeDtypeStruct((N, 1, C2), F32),
            jax.ShapeDtypeStruct((1, KB), F32),
        ),
        in_specs=[hbm, hbm, hbm, hbm, hbm, vmem, vmem, vmem, smem, smem],
        out_specs=(vmem, vmem, vmem),
        scratch_shapes=[
            V((2, T, KB), BF),
            V((N, KB, C2), BF),
            V((N, KB, C2), BF),
            V((N, C, KB), BF),
            V((N, C, KB), BF),
            V((KB, 128), F32),
            V((HB, 128), F32),
            V((N, 1, C2), F32),
            V((N, 1, C2), F32),
            V((1, KB), F32),
            V((1, KB), F32),
            V((N, 2, QTR, C3), F32),
            V((N, 2, QTR, C3), BF),
            V((N, 2, QTR, C3), BF),
            V((N, 2, QTR, C3), BF),
            V((N, 3, 2, SUB, C3), BF),
            V((N, 2, HALF, C3), BF),
            V((T, KB), F32),
            V((T, KB), BF),
            V((2, 3, BLK, KB), BF),
            V((BLK, KB), BF),
            V((BLK, KB), BF),
            V((N, 1, C2), F32),
            V((8, N, 1, C2), F32),
            V((4, N, 1, C2), F32),
            V((1, KB), F32),
            V((4, 1, KB), F32),
            V((8, 1, KB), F32),
            S((2,)),
            S((N, 2)),
            S((N,)),
            S, S,
            S((2, 3)), S((2, 3)),
            S((N, 2)), S((N, 2)),
            S((N, 2, 3)), S((N, 2, 3)),
            S((N, 2, 3)), S((N, 2, 3)),
            S((N, 2)), S((N, 2)),
            S((2, 3)), S((2, 3)),
            S, S,
            S((7,)), S((8,)),
            S((3,)), S((4,)),
            S((3,)), S((4,)),
            S((7,)), S((8,)),
        ],
        compiler_params=pltpu.CompilerParams(
            collective_id=0, has_side_effects=True, vmem_limit_bytes=56 * 2**20
        ),
        name="swiglu_back",
    )(
        tokens, out_grad, gate_weight, up_weight, down_weight,
        gate_step, up_step, down_step,
        outlier_in, outlier_hidden,
    )
    return pl.pallas_call(
        place,
        out_shape=(
            jax.ShapeDtypeStruct((BLK, KB), BF),
            jax.ShapeDtypeStruct((HB,), F32),
            jax.ShapeDtypeStruct((HB,), F32),
            jax.ShapeDtypeStruct((KB,), F32),
        ),
        in_specs=[vmem] * 3,
        out_specs=(vmem,) * 4,
        name="place",
    )(*results)


def solution(mesh):
    return jax.shard_map(
        shards,
        mesh=mesh,
        in_specs=(
            P(("dp", "dout"), "din"),
            P(("dp", "dout"), "din"),
            P("din", "dout"),
            P("din", "dout"),
            P("dout", "din"),
            P("dout"),
            P("dout"),
            P("din"),
            P("din"),
            P("dout"),
        ),
        out_specs=(P(("dp", "dout"), "din"), P("dout"), P("dout"), P("din")),
        check_vma=False,
    )
```
